32 devices in a mesh: parts: 2 (over x), dp: 2 (over core), tensor: 8 (over z, y).
Axes of the slice: x: 2, y: 2, z: 4, core: 2. Of those that a mesh axis runs over, the one named last changes fastest.
Arguments:
- home: bfloat16 [8192, 6144], P('tensor', ('parts', 'dp')), parts along dimension 1, as said below
- gain: bfloat16 [8192], replicated, may hold values from 0.099609375 to 1.8984375
- q_values: bfloat16 [8192, 2048], P(None, 'tensor')
- q_scales: float32 [64, 16], P(None, 'tensor'), may hold values from 0.5 to 2
- k_values: bfloat16 [256, 8192], P('tensor')
- k_scales: float32 [2, 64], replicated, may hold values from 0.5 to 2
- v_values: bfloat16 [256, 8192], P('tensor'), may hold values from -0.1875 to 0.1875
- v_scales: float32 [2, 64], replicated, may hold values from 0.5 to 2
- o_values: bfloat16 [2048, 8192], P('tensor'), may hold values from -0.1875 to 0.1875
- o_scales: float32 [16, 64], P('tensor'), may hold values from 0.5 to 2
- row_lengths: int32 [32], P('parts'), parts along dimension 0, may hold values from 1 to 192, as said below
- row_dest: int32 [32], P('parts'), parts along dimension 0, may hold values from 0 to 1, as said below
Outputs:
- attended: bfloat16 [8192, 3072], P('tensor', ('parts', 'dp')), parts along dimension 1
The draws below stay inside these ranges and needn't reach their ends.
There are 2 independent parts, one for each index of `parts`. The reference program is written for one: setup_inputs(seed, part) draws one part's arguments, and reference() takes and returns one part's arrays. A program takes and returns all parts, laid end to end along the dimension named above; an argument that names none is the same for every part. Nothing has to cross between parts.
Inputs may be any that keep to these rules, and one draw needn't show every extreme that they name: `row_lengths`: each group has exactly four rows bound for each group; their lengths add up to 384, and one of them has exactly 192 tokens. `row_dest`: each group sends four of its 8 rows to every group, itself included. `home`: slots past a row's length hold arbitrary finite values.
All inputs are finite; a program needn't handle non-finite values.
Results may differ from the reference program's by a relative error of at most 0.013.
Values may be sent and summed in bfloat16 or wider, within the bound.
No kernel may reach another device: no remote copies, remote signals or barrier semaphores. Data moves between devices by JAX's collectives and lax.ppermute only.
A program may use at most 128 MiB of HBM per device.

```python
import math
import jax
import jax.numpy as jnp
from jax import lax

D = 8192
HD = 128
HEADS_DEV = 2
GROUP = 8
HEADS = 16
KV_HEADS = 2
CAPT = 384
SLOT = 192
ROWS = 8
HOME = 1536
N_DP = 2
N_TENSOR = 8


def draw_home(key, part):
    key = jax.random.fold_in(key, 11)
    subkeys = jax.random.split(key, 3)
    columns = N_DP * HOME
    feature_scale = 10.0 ** (0.5 * jnp.arange(D, dtype=jnp.float32) / D + 0.5 * jax.random.uniform(subkeys[0], (D,)))
    token_scale = 10.0 ** jax.random.uniform(subkeys[1], (columns,))
    drawn_values = jax.random.normal(subkeys[2], (D, columns)) * feature_scale[:, None]
    return (drawn_values * token_scale[None, :]).astype(jnp.bfloat16)


def draw_q_values(key, part):
    key = jax.random.fold_in(key, 13)
    drawn_values = jax.random.normal(key, (D, HEADS * HD)) / math.sqrt(D)
    return drawn_values.astype(jnp.bfloat16)


def draw_k_values(key, part):
    key = jax.random.fold_in(key, 17)
    drawn_values = jax.random.normal(key, (KV_HEADS * HD, D)) / math.sqrt(D)
    return drawn_values.astype(jnp.bfloat16)


def deal_rows(key):
    key = jax.random.fold_in(key, 5)
    pair_keys = jax.random.split(key, N_DP * N_DP + N_DP)

    def one_pair(pair_key):
        cut_key, order_key = jax.random.split(pair_key)
        cut_points = jax.random.permutation(cut_key, SLOT - 1)[:2] + 1
        lower_cut = jnp.minimum(cut_points[0], cut_points[1])
        upper_cut = jnp.maximum(cut_points[0], cut_points[1])
        four_rows = jnp.stack([upper_cut * 0 + SLOT, lower_cut, upper_cut - lower_cut, SLOT - upper_cut]).astype(jnp.int32)
        return four_rows[jax.random.permutation(order_key, 4)]
    lengths = jax.vmap(one_pair)(pair_keys[:N_DP * N_DP]).reshape(N_DP, ROWS)
    targets = jnp.broadcast_to(jnp.repeat(jnp.arange(N_DP, dtype=jnp.int32), 4)[None, :], (N_DP, ROWS))

    def shuffle(shuffle_key, row_lengths, row_targets):
        row_order = jax.random.permutation(shuffle_key, ROWS)
        return (row_lengths[row_order], row_targets[row_order])
    lengths, targets = jax.vmap(shuffle)(pair_keys[N_DP * N_DP:], lengths, targets)
    return (lengths.reshape(-1).astype(jnp.int32), targets.reshape(-1).astype(jnp.int32))


def draw_row_lengths(key, part):
    return deal_rows(key)[0]


def draw_row_dest(key, part):
    return deal_rows(key)[1]


def with_spikes(values, stream_key, source, target, parts, factor):
    owner, partner = [(jnp.arange(values.shape[dim]) // (values.shape[dim] // parts)).reshape([-1 if axis == dim else 1 for axis in range(values.ndim)]) for dim in (source, target)]
    chosen = jax.random.permutation(stream_key, parts)[partner]
    strong = (owner == chosen) | (owner == (partner + parts // 2) % parts)
    return jnp.where(strong, factor * values, values)


def level_of(key, dims, cuts, smallest, largest):
    loudness, own = 1.0, jax.random.fold_in(key, 6)
    for dim, shards_of in cuts:
        heights = jnp.exp(jax.random.uniform(jax.random.fold_in(own, dim), (shards_of,), jnp.float32, smallest / len(cuts), largest / len(cuts)))
        loudness = loudness * jnp.repeat(heights, dims[dim] // shards_of).reshape([-1 if axis == dim else 1 for axis in range(len(dims))])
    return loudness


def bell_draw(stream_key, dims, deviation, reach, cuts=(), kind=jnp.bfloat16):
    result = jax.random.normal(stream_key, dims, jnp.float32) * deviation
    if len(cuts) > 0:
        result = level_of(stream_key, dims, cuts, -0.22, 0.18) * result
    return jnp.clip(result, min=-reach, max=reach).astype(kind)


def noise_with(rng, shape, width, bound, cuts, heavy, held_as=jnp.bfloat16):
    result = width * jax.random.normal(rng, shape, jnp.float32)
    if cuts:
        result = result * level_of(rng, shape, cuts, -0.22, 0.18)
    return jnp.clip(with_spikes(result, jax.random.fold_in(rng, 3), *heavy), -bound, bound).astype(held_as)


def setup_inputs(seed: int = 0, part: int = 0) -> dict:
    keys = jax.random.split(jax.random.key(seed), 13)
    part_splits = jax.random.split(jax.random.fold_in(keys[12], part), 13)
    home = draw_home(jax.random.fold_in(jax.random.fold_in(keys[12], part), 71), part)
    gain = jnp.clip(1.0 + 0.18 * jax.random.normal(keys[1], (D,), jnp.float32), 0.099609375, 1.8984375).astype(jnp.bfloat16)
    q_values = draw_q_values(jax.random.fold_in(keys[12], 71), part)
    q_scales = jnp.clip(jnp.exp(math.log(2.0) - 1.3862944 * jax.random.uniform(keys[3], (D // HD, HEADS), jnp.float32) ** level_of(keys[3], (D // HD, HEADS), ((1, 8),), -0.2, 0.2)), 0.5, 2.0)
    k_values = draw_k_values(jax.random.fold_in(keys[12], 71), part)
    k_scales = jnp.clip(jnp.exp(jax.random.uniform(keys[5], (KV_HEADS, D // HD), jnp.float32, math.log(0.5), math.log(2.0))), 0.5, 2.0)
    v_values = bell_draw(keys[6], (KV_HEADS * HD, D), (D // 9) ** -0.5, 0.1875, ((0, 8),))
    v_scales = jnp.clip(jnp.exp(jax.random.uniform(keys[7], (KV_HEADS, D // HD), jnp.float32, math.log(0.5), math.log(2.0))), 0.5, 2.0)
    o_values = noise_with(keys[8], (HEADS * HD, D), (HEADS * HD) ** -0.5, 0.1875, ((0, 8),), (0, 1, 8, 2.0))
    o_scales = jnp.clip(jnp.exp(math.log(2.0) - 1.3862944 * jax.random.uniform(keys[9], (HEADS, D // HD), jnp.float32) ** level_of(keys[9], (HEADS, D // HD), ((0, 8),), -0.2, 0.2)), 0.5, 2.0)
    row_lengths = draw_row_lengths(jax.random.fold_in(jax.random.fold_in(keys[12], part), 71), part)
    row_dest = draw_row_dest(jax.random.fold_in(jax.random.fold_in(keys[12], part), 71), part)
    return {"home": home, "gain": gain, "q_values": q_values, "q_scales": q_scales, "k_values": k_values, "k_scales": k_scales, "v_values": v_values, "v_scales": v_scales, "o_values": o_values, "o_scales": o_scales, "row_lengths": row_lengths, "row_dest": row_dest}


epsilon = 1e-06
rope_base = 1000000.0

def dequantize(stored, scales):
    row_repeat = stored.shape[0] // scales.shape[0]
    column_repeat = stored.shape[1] // scales.shape[1]
    spread = jnp.repeat(jnp.repeat(scales, row_repeat, axis=0), column_repeat, axis=1)
    return (stored.astype(jnp.float32) * spread).astype(jnp.bfloat16)

def row_layout(lengths, chosen, columns):
    live_taken = jnp.where(chosen, lengths, 0)
    finish = jnp.cumsum(live_taken, axis=1)
    row_begin = finish - live_taken
    places = jnp.arange(columns, dtype=jnp.int32)[None, :, None]
    inside = chosen[:, None, :] & (row_begin[:, None, :] <= places) & (places < finish[:, None, :])
    numbers = jnp.arange(lengths.shape[1], dtype=jnp.int32)[None, None, :]
    row_of = lax.optimization_barrier(jnp.sum(jnp.where(inside, numbers, 0), axis=2)).astype(jnp.int32)
    within = lax.optimization_barrier(jnp.sum(jnp.where(inside, places - row_begin[:, None, :], 0), axis=2)).astype(jnp.int32)
    return (row_of, within)

def rope_tables(position, head_size):
    half_size = head_size // 2
    frequency = rope_base ** (-2.0 * jnp.arange(half_size, dtype=jnp.float32) / head_size)
    phases = position.astype(jnp.float32)[:, None] * frequency[None, :]
    return (jnp.cos(phases), jnp.sin(phases))

def rotate(vectors, cosine, sine_table):
    half_size = vectors.shape[-1] // 2
    lower_half = vectors[..., :half_size]
    upper_half = vectors[..., half_size:]
    return jnp.concatenate([lower_half * cosine - upper_half * sine_table, upper_half * cosine + lower_half * sine_table], axis=-1)

def one_group(packed, row_keys, position, gain, q_weight, k_weight, v_weight, o_weight):
    tokens = packed.shape[1]
    wide_rows = packed.astype(jnp.float32)
    inverse = lax.rsqrt(lax.optimization_barrier(jnp.sum(wide_rows * wide_rows, axis=0)) / D + epsilon)
    normed = (wide_rows * inverse[None, :] * gain.astype(jnp.float32)[:, None]).astype(jnp.bfloat16)
    normed_rows = normed.T
    query_proj = jnp.dot(normed_rows, q_weight, preferred_element_type=jnp.float32).astype(jnp.bfloat16)
    key_proj = jnp.dot(normed_rows, k_weight.T, preferred_element_type=jnp.float32).astype(jnp.bfloat16)
    value_proj = jnp.dot(normed_rows, v_weight.T, preferred_element_type=jnp.float32).astype(jnp.bfloat16)
    cosine, sine_table = rope_tables(position, HD)
    rotated_q = rotate(query_proj.astype(jnp.float32).reshape(tokens, HEADS, HD), cosine[:, None, :], sine_table[:, None, :]).astype(jnp.bfloat16)
    rotated_k = rotate(key_proj.astype(jnp.float32).reshape(tokens, KV_HEADS, HD), cosine[:, None, :], sine_table[:, None, :]).astype(jnp.bfloat16)
    value_heads = value_proj.reshape(tokens, KV_HEADS, HD)
    column_index = jnp.arange(tokens, dtype=jnp.int32)
    allowed = (row_keys[:, None] == row_keys[None, :]) & (column_index[None, :] <= column_index[:, None])
    score_scale = 1.0 / math.sqrt(HD)

    def one_head(head_index):
        kv_index = head_index // GROUP
        query_head = lax.dynamic_index_in_dim(rotated_q, head_index, 1, keepdims=False)
        key_head = lax.dynamic_index_in_dim(rotated_k, kv_index, 1, keepdims=False)
        value_head = lax.dynamic_index_in_dim(value_heads, kv_index, 1, keepdims=False)
        scores = jnp.dot(query_head, key_head.T, preferred_element_type=jnp.float32) * score_scale
        scores = jnp.where(allowed, scores, -1e+30)
        highest = lax.optimization_barrier(jnp.max(scores, axis=1, keepdims=True))
        weights = jnp.exp(scores - highest)
        attention = (weights / lax.optimization_barrier(jnp.sum(weights, axis=1, keepdims=True))).astype(jnp.bfloat16)
        return jnp.dot(attention, value_head, preferred_element_type=jnp.float32).astype(jnp.bfloat16)
    contexts = lax.map(one_head, jnp.arange(HEADS, dtype=jnp.int32))
    context = contexts.transpose(1, 0, 2).reshape(tokens, HEADS * HD)
    context_groups = context.reshape(tokens, N_TENSOR, HEADS_DEV * HD).transpose(1, 0, 2)
    weight_groups = o_weight.reshape(N_TENSOR, HEADS_DEV * HD, D)

    def add_term(running, pieces):
        term_part = jnp.dot(pieces[0], pieces[1], preferred_element_type=jnp.float32).astype(jnp.bfloat16)
        term_part = lax.optimization_barrier(term_part)
        return (running + term_part.astype(jnp.float32), None)
    summed, _ = lax.scan(add_term, jnp.zeros((tokens, D), jnp.float32), (context_groups, weight_groups))
    return summed.T.astype(jnp.bfloat16)

def reference(home, gain, q_values, q_scales, k_values, k_scales, v_values, v_scales, o_values, o_scales, row_lengths, row_dest):
    all_lengths = row_lengths.reshape(N_DP, ROWS)
    all_dest = row_dest.reshape(N_DP, ROWS)
    q_weight = dequantize(q_values, q_scales)
    k_weight = dequantize(k_values, k_scales)
    v_weight = dequantize(v_values, v_scales)
    o_weight = dequantize(o_values, o_scales)
    home_groups = home.reshape(D, N_DP, HOME)
    results = []
    for target in range(N_DP):
        row_of, within = row_layout(all_lengths, all_dest == target, CAPT)
        packed = jnp.concatenate([home_groups[:, source][:, row_of[source] * SLOT + within[source]] for source in range(N_DP)], axis=1)
        row_keys = (jnp.arange(N_DP, dtype=jnp.int32)[:, None] * ROWS + row_of).reshape(-1)
        results.append(one_group(packed, row_keys, within.reshape(-1), gain, q_weight, k_weight, v_weight, o_weight))
    return jnp.concatenate(results, axis=1)
```

```python
import functools
import math

import jax
import jax.numpy as jnp
from jax import lax
from jax.experimental import pallas as pl
from jax.experimental.pallas import tpu as pltpu
from jax.sharding import PartitionSpec as P

D = 8192
HD = 128
BLOCKS = 4

epsilon = 1e-06
rope_base = 1000000.0

F32 = jnp.float32
BF16 = jnp.bfloat16
NN = (((1,), (0,)), ((), ()))
NT = (((1,), (1,)), ((), ()))
MIB = 1 << 20


def dot(a, b, dims=NN):
    return lax.dot_general(a, b, dims, preferred_element_type=F32)


def in_vmem():
    return pl.BlockSpec(memory_space=pltpu.VMEM)


def in_smem():
    return pl.BlockSpec(memory_space=pltpu.SMEM)


def row_facts(lens, dest, source, target, rows, slot):
    zero = jnp.int32(0)
    start, seen = zero, zero
    full = [zero, zero]
    short = [[zero, zero, zero] for _ in range(3)]
    for i in range(rows):
        mine = dest[source * rows + i] == target
        size = jnp.where(mine, lens[source * rows + i], 0)
        is_full = size == slot
        is_short = jnp.logical_and(mine, size != slot)
        full = [jnp.where(is_full, i, full[0]), jnp.where(is_full, start, full[1])]
        for k in range(3):
            hit = jnp.logical_and(is_short, seen == k)
            for e, value in enumerate((jnp.int32(i), start, size)):
                short[k][e] = jnp.where(hit, value, short[k][e])
        seen = seen + jnp.where(is_short, 1, 0)
        start = start + size
    return full, short


def qkv_pieces_kernel(chunks, width, place, q_ref, k_ref, v_ref, qs, ks, vs, *outs):
    unit = pl.program_id(0)
    quarter, head = place[0], place[1]
    part = k_ref.shape[0]
    for chunk in range(chunks):
        out = outs[chunk]
        for i in range(width // HD):
            rows = slice(chunk * width + i * HD, chunk * width + (i + 1) * HD)
            block = (unit * 4 + quarter) * (chunks * width // HD) + chunk * (width // HD) + i
            for h in range(q_ref.shape[1] // HD):
                cols = slice(h * HD, (h + 1) * HD)
                out[0, i * HD : (i + 1) * HD, cols] = (
                    q_ref[rows, cols].astype(F32) * qs[block, h]
                ).astype(BF16)
            lanes = slice(i * HD, (i + 1) * HD)
            out[0, width : width + part, lanes] = (
                k_ref[:, rows].astype(F32) * ks[head, block]
            ).astype(BF16)
            out[0, width + part : width + 2 * part, lanes] = (
                v_ref[:, rows].astype(F32) * vs[head, block]
            ).astype(BF16)
        if width < q_ref.shape[1]:
            out[0, width:, width:] = jnp.zeros((2 * part, q_ref.shape[1] - width), BF16)


def qkv_pieces(place, q_values, q_scales, k_values, k_scales, v_values, v_scales, units):
    own = q_values.shape[1]
    part = k_values.shape[0]
    quarter = q_values.shape[0] // units // 4
    width = min(quarter, 256)
    chunks = quarter // width
    shape = jax.ShapeDtypeStruct((units, width + 2 * part, own), BF16)
    grid_spec = pltpu.PrefetchScalarGridSpec(
        num_scalar_prefetch=1,
        grid=(units,),
        in_specs=[
            pl.BlockSpec((quarter, own), lambda i, s: (i * 4 + s[0], 0)),
            pl.BlockSpec((part, quarter), lambda i, s: (0, i * 4 + s[0])),
            pl.BlockSpec((part, quarter), lambda i, s: (0, i * 4 + s[0])),
            in_smem(),
            in_smem(),
            in_smem(),
        ],
        out_specs=[pl.BlockSpec((1, width + 2 * part, own), lambda i, s: (i, 0, 0))] * chunks,
    )
    return pl.pallas_call(
        functools.partial(qkv_pieces_kernel, chunks, width),
        grid_spec=grid_spec,
        out_shape=[shape] * chunks,
        name="qkv_pieces",
    )(place, q_values, k_values, v_values, q_scales, k_scales, v_scales)


def o_pieces_kernel(fq, place, o_ref, scales, out):
    target = pl.program_id(0)
    quarter = place[0]
    own = o_ref.shape[0]
    if o_ref.shape[1] == fq:
        first = (target * 4 + quarter) * fq
        for h in range(own // HD):
            for i in range(fq // HD):
                s = scales[h, first // HD + i]
                block = o_ref[h * HD : (h + 1) * HD, i * HD : (i + 1) * HD].astype(F32) * s
                out[0, i * HD : (i + 1) * HD, h * HD : (h + 1) * HD] = block.T.astype(BF16)
    else:
        for h in range(own // HD):
            total = jnp.zeros((fq, HD), F32)
            for i in range(4):
                s = scales[h, (target * 4 + i) * fq // HD]
                block = o_ref[h * HD : (h + 1) * HD, :].astype(F32).T[i * fq : (i + 1) * fq] * s
                total = jnp.where(quarter == i, block, total)
            out[0, :, h * HD : (h + 1) * HD] = total.astype(BF16)


def o_pieces(place, o_values, o_scales, ranks):
    own = o_values.shape[0]
    features = o_values.shape[1] // ranks
    fq = features // 4
    if fq % HD == 0:
        spec = pl.BlockSpec((own, fq), lambda i, s: (0, i * 4 + s[0]))
    else:
        spec = pl.BlockSpec((own, features), lambda i, s: (0, i))
    grid_spec = pltpu.PrefetchScalarGridSpec(
        num_scalar_prefetch=1,
        grid=(ranks,),
        in_specs=[spec, in_smem()],
        out_specs=pl.BlockSpec((1, fq, own), lambda i, s: (i, 0, 0)),
    )
    return pl.pallas_call(
        functools.partial(o_pieces_kernel, fq),
        grid_spec=grid_spec,
        out_shape=jax.ShapeDtypeStruct((ranks, fq, own), BF16),
        name="o_pieces",
    )(place, o_values, o_scales)


def deal_kernel(rows, slot, place, lens, dest, home, keep, send, squares, pos, pick, folded):
    step = pl.program_id(0)
    group, block = place[0], place[1]

    @pl.when(step == 0)
    def _():
        column = lax.broadcasted_iota(jnp.int32, (slot, 1), 0)
        lane = lax.broadcasted_iota(jnp.int32, (slot, rows * slot), 1)
        for turn in range(2):
            full, short = row_facts(lens, dest, group, group ^ turn, rows, slot)
            first = short[0][2]
            second = first + short[1][2]
            from_short = jnp.where(
                column < first,
                short[0][0] * slot + column,
                jnp.where(
                    column < second,
                    short[1][0] * slot + column - first,
                    short[2][0] * slot + column - second,
                ),
            )
            for kind, index in enumerate((full[0] * slot + column, from_short)):
                at = (turn * 2 + kind) * slot
                pick[at : at + slot, :] = jnp.where(lane == index, 1.0, 0.0).astype(BF16)
        _, short = row_facts(lens, dest, group ^ (block >> 1), group, rows, slot)
        first = short[0][2]
        second = first + short[1][2]
        begin = jnp.where(column < first, 0, jnp.where(column < second, first, second))
        place_in_row = column - jnp.where((block & 1) == 1, begin, 0)
        pos[...] = jnp.broadcast_to(place_in_row.astype(F32), pos.shape)
        folded[...] = jnp.zeros_like(folded)

    taken = dot(pick[...], home[...], NT)
    half = 2 * slot
    keep[...] = taken[:half].astype(BF16)
    send[...] = taken[half:].astype(BF16)
    total = folded[...]
    for i in range(taken.shape[1] // 128):
        part = taken[:, i * 128 : (i + 1) * 128]
        total = total + part * part
    folded[...] = total

    @pl.when(step == pl.num_programs(0) - 1)
    def _():
        sums = jnp.sum(folded[...].T, axis=0, keepdims=True)
        squares[...] = jnp.broadcast_to(sums, squares.shape)


def deal(place, lens, dest, home, rows, slot):
    features = home.shape[0]
    width = min(features, 256)
    tokens = BLOCKS * slot
    return pl.pallas_call(
        functools.partial(deal_kernel, rows, slot),
        grid=(features // width,),
        in_specs=[
            in_smem(),
            in_smem(),
            in_smem(),
            pl.BlockSpec((width, home.shape[1]), lambda i: (i, 0)),
        ],
        out_specs=[
            pl.BlockSpec((tokens // 2, width), lambda i: (0, i)),
            pl.BlockSpec((tokens // 2, width), lambda i: (0, i)),
            pl.BlockSpec((8, tokens), lambda i: (0, 0)),
            pl.BlockSpec((slot, 128), lambda i: (0, 0)),
        ],
        out_shape=[
            jax.ShapeDtypeStruct((tokens // 2, features), BF16),
            jax.ShapeDtypeStruct((tokens // 2, features), BF16),
            jax.ShapeDtypeStruct((8, tokens), F32),
            jax.ShapeDtypeStruct((slot, 128), F32),
        ],
        scratch_shapes=[
            pltpu.VMEM((tokens, rows * slot), BF16),
            pltpu.VMEM((tokens, 128), F32),
        ],
        compiler_params=pltpu.CompilerParams(vmem_limit_bytes=32 * MIB),
        name="deal",
    )(place, lens, dest, home)


def project_kernel(units, chunks, width, place, squares, gain, keep, got, keep2, got2, *rest):
    weights = rest[: 4 * chunks]
    q_outs = rest[4 * chunks : 4 * chunks + units]
    kv_outs = rest[4 * chunks + units : 4 * chunks + 2 * units]
    normed, total = rest[4 * chunks + 2 * units :]
    unit, side, quarter = place[0], place[1], place[2]
    half, features = keep.shape
    tokens = 2 * half
    slot = tokens // BLOCKS
    inverse = lax.rsqrt(squares[...] / D + epsilon).T[:, :1]
    for at, pair in ((side, (keep, got)), (1 - side, (keep2, got2))):
        lanes = pl.ds(pl.multiple_of(at * features, 128), features)
        own_gain = gain[:, lanes]
        for e, ref in enumerate(pair):
            rows = slice(e * half, (e + 1) * half)
            normed[rows, lanes] = (ref[...].astype(F32) * inverse[rows] * own_gain).astype(BF16)

    def lanes_of(turn, chunk):
        at = (quarter ^ turn) * (chunks * width) + chunk * width
        return pl.ds(pl.multiple_of(at, 128), width)

    pieces = [(r, c) for r in range(4) for c in range(chunks)]

    def hand_out(group, outs, cols):
        for k in range(units):
            target = unit ^ k

            def write(out=outs[k], target=target):
                rows = pl.ds(pl.multiple_of((target & 3) * slot, 16), slot)
                out[:, cols] = total[rows, :].astype(BF16)

            if units == BLOCKS:
                write()
            else:
                pl.when((target >> 2) == group)(write)

    own = total.shape[1]
    for group in range(units // BLOCKS):
        value = None
        for r, c in pieces:
            w = weights[r * chunks + c]
            w = w[group * 4 : group * 4 + 4, width:, :width]
            w = w.reshape(4 * w.shape[1], width)
            term = dot(normed[:, lanes_of(r, c)], w, NT)
            value = term if value is None else value + term
        total[...] = value
        hand_out(group, kv_outs, slice(0, own))
        for s in range(4):
            value = None
            for r, c in pieces:
                w = weights[r * chunks + c][group * 4 + s, :width, :]
                term = dot(normed[:, lanes_of(r, c)], w)
                value = term if value is None else value + term
            total[...] = value
            hand_out(group, q_outs, slice(s * own, (s + 1) * own))


def project(place, squares, gain, keep, got, keep2, got2, weights, units, chunks, width):
    half, features = keep.shape
    slot = half // 2
    own = weights[0].shape[2]
    kv = 4 * (weights[0].shape[1] - width)
    outs = pl.pallas_call(
        functools.partial(project_kernel, units, chunks, width),
        in_specs=[in_smem()] + [in_vmem()] * (6 + len(weights)),
        out_specs=[in_vmem()] * (2 * units),
        out_shape=[jax.ShapeDtypeStruct((slot, 4 * own), BF16)] * units
        + [jax.ShapeDtypeStruct((slot, kv), BF16)] * units,
        scratch_shapes=[
            pltpu.VMEM((2 * half, 2 * features), BF16),
            pltpu.VMEM((2 * half, own), F32),
        ],
        compiler_params=pltpu.CompilerParams(vmem_limit_bytes=40 * MIB),
        name="project",
    )(place, squares, gain, keep, got, keep2, got2, *weights)
    return outs[:units], outs[units:]


def key_value_kernel(units, *refs):
    parts, (cosine, sine), out = refs[:units], refs[units : units + 2], refs[units + 2]
    value = parts[0][...].astype(F32)
    for part in parts[1:]:
        value = value + part[...].astype(F32)
    value = value.astype(BF16).astype(F32)
    part = value.shape[1] // 8
    keys = [value[:, 2 * i * part : (2 * i + 1) * part] for i in range(4)]
    values = [value[:, (2 * i + 1) * part : (2 * i + 2) * part] for i in range(4)]
    turned = []
    for h in range(2):
        low, high = keys[2 * h], keys[2 * h + 1]
        turned.append(low * cosine[...] - high * sine[...])
        turned.append(high * cosine[...] + low * sine[...])
    out[...] = jnp.concatenate(turned + values, axis=1).astype(BF16)


def key_value(parts, cosine, sine):
    return pl.pallas_call(
        functools.partial(key_value_kernel, len(parts)),
        in_specs=[in_vmem()] * (len(parts) + 2),
        out_specs=in_vmem(),
        out_shape=jax.ShapeDtypeStruct(parts[0].shape, BF16),
        name="key_value",
    )(*parts, cosine, sine)


def attend_kernel(units, rows, slot, place, lens, dest, cosine, sine, own_kv, other_kv, *refs):
    parts, out = refs[:units], refs[units]
    group, block, side = place[0], place[1], place[2]
    _, short = row_facts(lens, dest, group ^ (block >> 1), group, rows, slot)
    many = (block & 1) == 1
    first = jnp.where(many, short[0][2], slot)
    second = jnp.where(many, first + short[1][2], slot)

    def segment(shape, axis):
        at = lax.broadcasted_iota(jnp.int32, shape, axis)
        return jnp.where(at >= first, 1, 0) + jnp.where(at >= second, 1, 0)

    shape = (slot, slot)
    allowed = jnp.logical_and(
        segment(shape, 0) == segment(shape, 1),
        lax.broadcasted_iota(jnp.int32, shape, 1) <= lax.broadcasted_iota(jnp.int32, shape, 0),
    )
    mine, theirs = own_kv[...].astype(F32), other_kv[...].astype(F32)
    even = jnp.where(side == 0, mine, theirs)
    odd = jnp.where(side == 0, theirs, mine)
    part = HD // 4
    heads = []
    for h in range(4):
        pieces = []
        for b in range(2):
            at = slice((2 * h + b) * part, (2 * h + b + 1) * part)
            pieces += [even[:, at], odd[:, at]]
        heads.append(jnp.concatenate(pieces, axis=1).astype(BF16))
    cos, sin = cosine[...], sine[...]
    scale = 1.0 / math.sqrt(HD)
    count = out.shape[1] // HD
    for head in range(count):
        at = slice(head * HD, (head + 1) * HD)
        query = parts[0][:, at].astype(F32)
        for ref in parts[1:]:
            query = query + ref[:, at].astype(F32)
        query = query.astype(BF16).astype(F32)
        swapped = jnp.concatenate([query[:, HD // 2 :], query[:, : HD // 2]], axis=1)
        query = (query * cos + swapped * sin).astype(BF16)
        kv = head // (count // 2)
        scores = dot(query, heads[kv], NT) * scale
        scores = jnp.where(allowed, scores, -1e30)
        weights = jnp.exp(scores - jnp.max(scores, axis=1, keepdims=True))
        attention = (weights / jnp.sum(weights, axis=1, keepdims=True)).astype(BF16)
        out[:, at] = dot(attention, heads[2 + kv]).astype(BF16)


def attend(place, lens, dest, cosine, sine, own_kv, other_kv, parts, rows, slot):
    return pl.pallas_call(
        functools.partial(attend_kernel, len(parts), rows, slot),
        in_specs=[in_smem()] * 3 + [in_vmem()] * (4 + len(parts)),
        out_specs=in_vmem(),
        out_shape=jax.ShapeDtypeStruct(parts[0].shape, BF16),
        name="attend",
    )(place, lens, dest, cosine, sine, own_kv, other_kv, *parts)


def output_kernel(units, rows, slot, place, lens, dest, *refs):
    weights = refs[:4]
    mine, theirs = refs[4 : 4 + units], refs[4 + units : 4 + 2 * units]
    out, context, order = refs[4 + 2 * units :]
    unit, side, quarter, group = place[0], place[1], place[2], place[3]
    own = weights[0].shape[2]
    tokens = BLOCKS * slot
    for k in range(units):
        source = unit ^ k
        at_rows = pl.ds(pl.multiple_of((source & 3) * slot, 16), slot)
        for pieces, y in ((mine, side), (theirs, 1 - side)):
            for s in range(4):
                rank = ((source >> 2) * 4 + s) * 2 + y
                context[at_rows, pl.ds(pl.multiple_of(rank * own, 128), own)] = pieces[k][
                    :, s * own : (s + 1) * own
                ]
    half = 2 * slot
    column = lax.broadcasted_iota(jnp.int32, (1, half), 1)
    for source in range(2):
        full, short = row_facts(lens, dest, source, group, rows, slot)
        index = column - full[1]
        done = jnp.int32(0)
        for k in range(3):
            inside = jnp.logical_and(
                column >= short[k][1], column < short[k][1] + short[k][2]
            )
            index = jnp.where(inside, slot + done + column - short[k][1], index)
            done = done + short[k][2]
        index = index + (group ^ source) * half
        row = lax.broadcasted_iota(jnp.int32, (tokens, half), 0)
        order[:, source * half : (source + 1) * half] = jnp.where(
            row == index, 1.0, 0.0
        ).astype(BF16)
    ranks, fq = weights[0].shape[:2]
    for r in range(4):
        value = None
        for rank in range(ranks):
            term = dot(weights[r][rank], context[:, rank * own : (rank + 1) * own], NT)
            value = term if value is None else value + term
        at = pl.multiple_of((quarter ^ r) * fq, 16)
        out[pl.ds(at, fq), :] = dot(value.astype(BF16), order[...]).astype(BF16)


def output(place, lens, dest, weights, mine, theirs, rows, slot):
    units = len(mine)
    ranks, fq, own = weights[0].shape
    tokens = BLOCKS * slot
    return pl.pallas_call(
        functools.partial(output_kernel, units, rows, slot),
        in_specs=[in_smem()] * 3 + [in_vmem()] * (4 + 2 * units),
        out_specs=in_vmem(),
        out_shape=jax.ShapeDtypeStruct((4 * fq, tokens), BF16),
        scratch_shapes=[
            pltpu.VMEM((tokens, ranks * own), BF16),
            pltpu.VMEM((tokens, tokens), BF16),
        ],
        compiler_params=pltpu.CompilerParams(vmem_limit_bytes=48 * MIB),
        name="output",
    )(place, lens, dest, *weights, *mine, *theirs)


def swap(value, axis, mask=1):
    size = lax.axis_size(axis)
    return lax.ppermute(value, axis, [(i, i ^ mask) for i in range(size)])


def all_quarters(value):
    across = swap(value, "parts")
    return [value, swap(value, "dp"), across, swap(across, "dp")]


def body(
    home,
    gain,
    q_values,
    q_scales,
    k_values,
    k_scales,
    v_values,
    v_scales,
    o_values,
    o_scales,
    row_lengths,
    row_dest,
):
    ranks = lax.axis_size("tensor")
    units = ranks // 2
    rank = lax.axis_index("tensor")
    unit, side = rank >> 1, rank & 1
    group = lax.axis_index("dp")
    quarter = (lax.axis_index("parts") & 1) * 2 + group
    block = unit & (BLOCKS - 1)
    features = home.shape[0]
    rows = row_lengths.shape[0] // 2
    slot = home.shape[1] // rows
    half = 2 * slot

    def places(*values):
        return jnp.stack([jnp.asarray(v, jnp.int32) for v in values])

    columns = [[2 * u + y for u in range(units)] for y in range(2)]
    kv_head = rank * k_values.shape[0] // HD
    pieces = qkv_pieces(
        places(quarter, kv_head),
        q_values,
        q_scales,
        k_values,
        k_scales,
        v_values,
        v_scales,
        units,
    )
    chunks = len(pieces)
    width = D // units // 4 // chunks
    by_chunk = []
    for piece in pieces:
        moved = lax.all_to_all(
            piece, "tensor", split_axis=0, concat_axis=0, tiled=True, axis_index_groups=columns
        )
        by_chunk.append(all_quarters(moved))
    weights = [by_chunk[c][r] for r in range(4) for c in range(chunks)]

    keep, send, squares, pos = deal(
        places(group, block), row_lengths, row_dest, home, rows, slot
    )
    got = swap(send, "dp")
    keep2 = swap(keep, "tensor")
    got2 = lax.ppermute(
        send, ("dp", "tensor"), [(i, i ^ (ranks + 1)) for i in range(2 * ranks)]
    )
    bit = 1
    while bit < ranks:
        squares = squares + swap(squares, "tensor", bit)
        bit *= 2
    squares = jnp.concatenate([squares[:, :half], swap(squares[:, half:], "dp")], axis=1)

    own_gain = lax.dynamic_slice_in_dim(
        gain.astype(F32), unit * 2 * features, 2 * features
    ).reshape(1, -1)
    q_parts, kv_parts = project(
        places(unit, side, quarter),
        squares,
        own_gain,
        keep,
        got,
        keep2,
        got2,
        weights,
        units,
        chunks,
        width,
    )
    kv_parts = [kv_parts[0]] + [swap(kv_parts[k], "tensor", 2 * k) for k in range(1, units)]
    q_parts = [q_parts[0]] + [swap(q_parts[k], "tensor", 2 * k) for k in range(1, units)]

    frequency = rope_base ** (-2.0 * jnp.arange(HD // 2, dtype=F32) / HD)
    phases = pos[:, :1] * frequency[None, :]
    cosine, sine = jnp.cos(phases), jnp.sin(phases)
    part = HD // 4
    own_cos = lax.dynamic_slice_in_dim(cosine, side * part, part, 1)
    own_sin = lax.dynamic_slice_in_dim(sine, side * part, part, 1)
    own_kv = key_value(kv_parts, own_cos, own_sin)
    other_kv = swap(own_kv, "tensor")
    context = attend(
        places(group, block, side),
        row_lengths,
        row_dest,
        jnp.concatenate([cosine, cosine], axis=1),
        jnp.concatenate([-sine, sine], axis=1),
        own_kv,
        other_kv,
        q_parts,
        rows,
        slot,
    )

    o_moved = lax.all_to_all(
        o_pieces(places(quarter), o_values, o_scales, ranks),
        "tensor",
        split_axis=0,
        concat_axis=0,
        tiled=True,
    )
    o_weights = all_quarters(o_moved)
    mine = [context] + [swap(context, "tensor", 2 * k) for k in range(1, units)]
    theirs = [swap(value, "tensor") for value in mine]
    return output(
        places(unit, side, quarter, group),
        row_lengths,
        row_dest,
        o_weights,
        mine,
        theirs,
        rows,
        slot,
    )


def solution(mesh):
    in_specs = (
        P("tensor", ("parts", "dp")),
        P(),
        P(None, "tensor"),
        P(None, "tensor"),
        P("tensor", None),
        P(),
        P("tensor", None),
        P(),
        P("tensor", None),
        P("tensor", None),
        P("parts"),
        P("parts"),
    )
    out_specs = P("tensor", ("parts", "dp"))
    return jax.shard_map(body, mesh=mesh, in_specs=in_specs, out_specs=out_specs, check_vma=False)
```

```python
import functools
import math

import jax
import jax.numpy as jnp
from jax import lax
from jax.experimental import pallas as pl
from jax.experimental.pallas import tpu as pltpu
from jax.sharding import PartitionSpec as P

D = 8192
HD = 128
BLOCKS = 4

epsilon = 1e-06
rope_base = 1000000.0

F32 = jnp.float32
BF16 = jnp.bfloat16
NN = (((1,), (0,)), ((), ()))
NT = (((1,), (1,)), ((), ()))
TN = (((0,), (0,)), ((), ()))
VMEM = 58 << 20


def dot(a, b, dims=NN):
    return lax.dot_general(a, b, dims, preferred_element_type=F32)


def in_vmem():
    return pl.BlockSpec(memory_space=pltpu.VMEM)


def in_smem():
    return pl.BlockSpec(memory_space=pltpu.SMEM)


def anywhere():
    return pl.BlockSpec(memory_space=pltpu.HBM)


def start_copies(pairs, sems, first=0):
    copies = [
        pltpu.make_async_copy(source, target, sems.at[first + i])
        for i, (source, target) in enumerate(pairs)
    ]
    for copy in copies:
        copy.start()
    return copies


def aligned(value, size):
    return pl.ds(pl.multiple_of(value, size), size)


GROUP, UNIT, SIDE, QUARTER, KV_HEAD = range(5)


def row_facts(lens, dest, source, target, rows, slot):
    zero = jnp.int32(0)
    start, seen = zero, zero
    full = [zero, zero]
    short = [[zero, zero, zero] for _ in range(3)]
    for i in range(rows):
        mine = dest[source * rows + i] == target
        size = jnp.where(mine, lens[source * rows + i], 0)
        is_full = size == slot
        is_short = jnp.logical_and(mine, size != slot)
        full = [jnp.where(is_full, i, full[0]), jnp.where(is_full, start, full[1])]
        for k in range(3):
            hit = jnp.logical_and(is_short, seen == k)
            for e, value in enumerate((jnp.int32(i), start, size)):
                short[k][e] = jnp.where(hit, value, short[k][e])
        seen = seen + jnp.where(is_short, 1, 0)
        start = start + size
    return full, short


def pieces_kernel(units, place, qs, ks, vs, os, q_hbm, k_hbm, v_hbm, o_hbm, *rest):
    outs, o_out = rest[:units], rest[units]
    q_buf, k_buf, v_buf, o_buf, pieces, o_pieces, in_sems, out_sems = rest[units + 1 :]
    unit, quarter, head = place[UNIT], place[QUARTER], place[KV_HEAD]
    _, size, own = q_buf.shape
    part = k_buf.shape[1]
    width = min(size, own)
    ranks, o_rows, features = o_pieces.shape
    copies = []
    for k in range(units):
        at = ((unit ^ k) * 4 + quarter) * size
        copies.append(
            start_copies(
                [
                    (q_hbm.at[aligned(at, size)], q_buf.at[k]),
                    (k_hbm.at[:, aligned(at, size)], k_buf.at[k]),
                    (v_hbm.at[:, aligned(at, size)], v_buf.at[k]),
                ],
                in_sems,
                3 * k,
            )
        )
    (o_copy,) = start_copies(
        [(o_hbm.at[aligned(quarter * o_rows, o_rows)], o_buf)], in_sems, 3 * units
    )
    sent = []
    for k in range(units):
        for copy in copies[k]:
            copy.wait()
        base = ((unit ^ k) * 4 + quarter) * (size // HD)
        for i in range(size // HD):
            rows = slice(i * HD, (i + 1) * HD)
            for h in range(own // HD):
                cols = slice(h * HD, (h + 1) * HD)
                scaled = q_buf[k, rows, cols].astype(F32) * qs[h, base + i]
                pieces[k, rows, cols] = scaled.astype(BF16)
            turn, lane = divmod(i * HD, width)
            at = size + 2 * part * turn
            lanes = slice(lane, lane + HD)
            pieces[k, at : at + part, lanes] = (
                k_buf[k, :, rows].astype(F32) * ks[head, base + i]
            ).astype(BF16)
            pieces[k, at + part : at + 2 * part, lanes] = (
                v_buf[k, :, rows].astype(F32) * vs[head, base + i]
            ).astype(BF16)
        if width < own:
            pieces[k, size:, width:] = jnp.zeros((2 * part, own - width), BF16)
        sent += start_copies([(pieces.at[k], outs[k])], out_sems, k)
    o_copy.wait()
    o_head = quarter * o_rows // HD
    for rank in range(ranks):
        for i in range(features // HD):
            block = rank * (features // HD) + i
            scaled = o_buf[:, block * HD : (block + 1) * HD].astype(F32) * os[o_head, block]
            o_pieces[rank, :, i * HD : (i + 1) * HD] = scaled.astype(BF16)
    sent += start_copies([(o_pieces, o_out)], out_sems, units)
    for copy in sent:
        copy.wait()


def weight_pieces(
    place, q_values, q_scales, k_values, k_scales, v_values, v_scales, o_values, o_scales, ranks
):
    units = ranks // 2
    o_shape = (ranks, o_values.shape[0] // 4, o_values.shape[1] // ranks)
    own = q_values.shape[1]
    part = k_values.shape[0]
    size = q_values.shape[0] // units // 4
    rows = size + 2 * part * max(1, size // own)
    outs = pl.pallas_call(
        functools.partial(pieces_kernel, units),
        in_specs=[in_smem()] * 5 + [anywhere()] * 4,
        out_specs=[anywhere()] * (units + 1),
        out_shape=[jax.ShapeDtypeStruct((rows, own), BF16)] * units
        + [jax.ShapeDtypeStruct(o_shape, BF16)],
        scratch_shapes=[
            pltpu.VMEM((units, size, own), BF16),
            pltpu.VMEM((units, part, size), BF16),
            pltpu.VMEM((units, part, size), BF16),
            pltpu.VMEM((o_shape[1], o_values.shape[1]), BF16),
            pltpu.VMEM((units, rows, own), BF16),
            pltpu.VMEM(o_shape, BF16),
            pltpu.SemaphoreType.DMA((3 * units + 1,)),
            pltpu.SemaphoreType.DMA((units + 1,)),
        ],
        compiler_params=pltpu.CompilerParams(vmem_limit_bytes=VMEM),
        name="weight_pieces",
    )(place, q_scales.T, k_scales, v_scales, o_scales, q_values, k_values, v_values, o_values)
    return outs[:units], outs[units]


def deal_kernel(rows, slot, count, place, lens, dest, home, *rest):
    keep, send, pos, pick = rest[count:]
    step = pl.program_id(0)
    group, block = place[GROUP], place[UNIT] & (BLOCKS - 1)

    @pl.when(step == 0)
    def _():
        column = lax.broadcasted_iota(jnp.int32, (slot, 1), 0)
        lane = lax.broadcasted_iota(jnp.int32, (slot, rows * slot), 1)
        for turn in range(2):
            full, short = row_facts(lens, dest, group, group ^ turn, rows, slot)
            first = short[0][2]
            second = first + short[1][2]
            from_short = jnp.where(
                column < first,
                short[0][0] * slot + column,
                jnp.where(
                    column < second,
                    short[1][0] * slot + column - first,
                    short[2][0] * slot + column - second,
                ),
            )
            for kind, index in enumerate((full[0] * slot + column, from_short)):
                at = (turn * 2 + kind) * slot
                pick[at : at + slot, :] = jnp.where(lane == index, 1.0, 0.0).astype(BF16)
        _, short = row_facts(lens, dest, group ^ (block >> 1), group, rows, slot)
        first = short[0][2]
        second = first + short[1][2]
        begin = jnp.where(column < first, 0, jnp.where(column < second, first, second))
        place_in_row = column - jnp.where((block & 1) == 1, begin, 0)
        pos[...] = jnp.broadcast_to(place_in_row.astype(F32), pos.shape)

    taken = dot(pick[...], home[...], NT)
    half = 2 * slot
    keep[...] = taken[:half].astype(BF16)
    send[...] = taken[half:].astype(BF16)


def deal(place, lens, dest, home, rows, slot, after):
    features = home.shape[0]
    width = min(features, 256)
    tokens = BLOCKS * slot
    return pl.pallas_call(
        functools.partial(deal_kernel, rows, slot, len(after)),
        grid=(features // width,),
        in_specs=[
            in_smem(),
            in_smem(),
            in_smem(),
            pl.BlockSpec((width, home.shape[1]), lambda i: (i, 0)),
        ]
        + [anywhere()] * len(after),
        out_specs=[
            pl.BlockSpec((tokens // 2, width), lambda i: (0, i)),
            pl.BlockSpec((tokens // 2, width), lambda i: (0, i)),
            pl.BlockSpec((slot, 128), lambda i: (0, 0)),
        ],
        out_shape=[
            jax.ShapeDtypeStruct((tokens // 2, features), BF16),
            jax.ShapeDtypeStruct((tokens // 2, features), BF16),
            jax.ShapeDtypeStruct((slot, 128), F32),
        ],
        scratch_shapes=[
            pltpu.VMEM((tokens, rows * slot), BF16),
        ],
        compiler_params=pltpu.CompilerParams(vmem_limit_bytes=VMEM),
        name="deal",
    )(place, lens, dest, home, *after)


def collect_kernel(count, extra, *refs):
    tokens, pieces = refs[:4], refs[4 : 4 + count]
    out, sums = refs[4 + count + extra : 6 + count + extra]
    x_buf, buf, x_sems, sems, out_sems = refs[-5:]
    copies = start_copies([(ref, buf.at[k]) for k, ref in enumerate(pieces)], sems)
    x_copies = start_copies([(ref, x_buf.at[i]) for i, ref in enumerate(tokens)], x_sems)
    sent = []
    for k, copy in enumerate(copies):
        copy.wait()
        sent += start_copies([(buf.at[k], out.at[k])], out_sems, k)
    _, half, features = x_buf.shape
    for i in range(2):
        total = None
        for j in (i, i + 2):
            x_copies[j].wait()
            for at in range(features // 128):
                piece = x_buf[j, :, at * 128 : (at + 1) * 128].astype(F32)
                total = piece * piece if total is None else total + piece * piece
        sums[:, i * half : (i + 1) * half] = jnp.broadcast_to(
            jnp.sum(total.T, axis=0, keepdims=True), (8, half)
        )
    for copy in sent:
        copy.wait()


def collect(tokens, pieces, after):
    count = len(pieces)
    half, features = tokens[0].shape
    return pl.pallas_call(
        functools.partial(collect_kernel, count, len(after)),
        in_specs=[anywhere()] * (4 + count + len(after)),
        out_specs=[anywhere(), in_vmem()],
        out_shape=[
            jax.ShapeDtypeStruct((count, *pieces[0].shape), BF16),
            jax.ShapeDtypeStruct((8, 2 * half), F32),
        ],
        scratch_shapes=[
            pltpu.VMEM((4, half, features), BF16),
            pltpu.VMEM((count, *pieces[0].shape), BF16),
            pltpu.SemaphoreType.DMA((4,)),
            pltpu.SemaphoreType.DMA((count,)),
            pltpu.SemaphoreType.DMA((count,)),
        ],
        compiler_params=pltpu.CompilerParams(vmem_limit_bytes=VMEM),
        name="collect",
    )(*tokens, *pieces, *after)


def gate_kernel(*refs):
    pass


def gate(through, after):
    count = len(through)
    return pl.pallas_call(
        gate_kernel,
        in_specs=[anywhere()] * (count + len(after)),
        out_specs=[anywhere()] * count,
        out_shape=[jax.ShapeDtypeStruct(value.shape, value.dtype) for value in through],
        input_output_aliases={i: i for i in range(count)},
        compiler_params=pltpu.CompilerParams(vmem_limit_bytes=VMEM),
        name="gate",
    )(*through, *after)


def normalize_kernel(units, place, *rest):
    squares, (gain, keep, got, keep2, got2) = rest[:units], rest[units : units + 5]
    out, x_buf, normed, x_sems, out_sems = rest[units + 5 :]
    side = place[SIDE]
    _, half, features = x_buf.shape
    copies = start_copies(
        [(ref, x_buf.at[i]) for i, ref in enumerate((keep, got, keep2, got2))], x_sems
    )
    total = squares[0][...]
    for ref in squares[1:]:
        total = total + ref[...]
    inverse = lax.rsqrt(total / D + epsilon).T[:, :1]
    sent = []
    for i in range(4):
        at = side if i < 2 else 1 - side
        lanes = aligned(at * features, features)
        rows = slice((i & 1) * half, ((i & 1) + 1) * half)
        copies[i].wait()
        wide_rows = x_buf[i].astype(F32)
        normed[i] = (wide_rows * inverse[rows] * gain[:, lanes]).astype(BF16)
        sent += start_copies([(normed.at[i], out.at[rows, lanes])], out_sems, i)
    for copy in sent:
        copy.wait()


def normalize(place, squares, gain, keep, got, keep2, got2):
    half, features = keep.shape
    return pl.pallas_call(
        functools.partial(normalize_kernel, len(squares)),
        in_specs=[in_smem()] + [in_vmem()] * (len(squares) + 1) + [anywhere()] * 4,
        out_specs=anywhere(),
        out_shape=jax.ShapeDtypeStruct((2 * half, 2 * features), BF16),
        scratch_shapes=[
            pltpu.VMEM((4, half, features), BF16),
            pltpu.VMEM((4, half, features), BF16),
            pltpu.SemaphoreType.DMA((4,)),
            pltpu.SemaphoreType.DMA((4,)),
        ],
        compiler_params=pltpu.CompilerParams(vmem_limit_bytes=VMEM),
        name="normalize",
    )(place, *squares, gain, keep, got, keep2, got2)


def project_kernel(units, place, normed, *rest):
    own_pieces, weights, outs = rest[:4], rest[4:8], rest[8 : 8 + units]
    weight, tokens, buf, x_sem, w_sems, out_sems = rest[8 + units :]
    unit, quarter = place[UNIT], place[QUARTER]
    count, wide = tokens.shape
    slot = count // BLOCKS
    own = weight.shape[3]
    size = wide // 4
    width = min(size, own)
    part = (weight.shape[2] - size) // (size // width)
    (x_copy,) = start_copies([(normed, tokens)], x_sem)
    copies = start_copies(
        [
            (
                weights[r].at[k - 1] if k else own_pieces[r],
                weight.at[quarter ^ r, (k >> 2) * 4 + ((unit ^ k) & 3)],
            )
            for k in range(units)
            for r in range(4)
        ],
        w_sems,
    )
    x_copy.wait()
    sent = []

    def hand_out(group, cols, index):
        for k in range(4 * group, 4 * group + 4):
            rows = aligned(((unit ^ k) & 3) * slot, slot)
            pair = (buf.at[group, rows, cols], outs[k].at[:, cols])
            sent.extend(start_copies([pair], out_sems, 5 * k + index))

    for group in range(units // BLOCKS):
        for k in range(4 * group, 4 * group + 4):
            for r in range(4):
                copies[k * 4 + r].wait()
            s = (unit ^ k) & 3
            value = None
            for q in range(4):
                term = dot(tokens[:, q * size : (q + 1) * size], weight[q, group * 4 + s, :size])
                value = term if value is None else value + term
            cols = aligned(s * own, own)
            buf[group, :, cols] = value.astype(BF16)
            hand_out(group, cols, k & 3)
        sources = slice(group * 4, group * 4 + 4)
        value = None
        for q in range(4):
            for e in range(size // width):
                at = q * size + e * width
                first = size + e * part
                middle, last = first + part // 2, first + part
                w = jnp.concatenate(
                    [
                        weight[q, sources, first:middle, :width].reshape(2 * part, width),
                        weight[q, sources, middle:last, :width].reshape(2 * part, width),
                    ],
                    axis=0,
                )
                term = dot(tokens[:, at : at + width], w, NT)
                value = term if value is None else value + term
        buf[group, :, 4 * own :] = value.astype(BF16)
        hand_out(group, pl.ds(4 * own, 4 * part), 4)
    for copy in sent:
        copy.wait()


def project(place, normed, own_pieces, weights, units):
    tokens, wide = normed.shape
    slot = tokens // BLOCKS
    rows, own = own_pieces[0].shape
    size = wide // 4
    part = (rows - size) // (size // min(size, own))
    groups = units // BLOCKS
    outs = pl.pallas_call(
        functools.partial(project_kernel, units),
        in_specs=[in_smem()] + [anywhere()] * 9,
        out_specs=[anywhere()] * units,
        out_shape=[jax.ShapeDtypeStruct((slot, 4 * own + 4 * part), BF16)] * units,
        scratch_shapes=[
            pltpu.VMEM((4, units, rows, own), BF16),
            pltpu.VMEM((tokens, wide), BF16),
            pltpu.VMEM((groups, tokens, 4 * own + 4 * part), BF16),
            pltpu.SemaphoreType.DMA((1,)),
            pltpu.SemaphoreType.DMA((4 * units,)),
            pltpu.SemaphoreType.DMA((5 * units,)),
        ],
        compiler_params=pltpu.CompilerParams(vmem_limit_bytes=VMEM),
        name="project",
    )(place, normed, *own_pieces, *weights)
    return outs


def key_value_kernel(units, cosine, sine, *refs):
    parts, (out, buf, sems) = refs[:units], refs[units:]
    wide = parts[0].shape[1] - buf.shape[2]
    copies = start_copies([(ref.at[:, wide:], buf.at[k]) for k, ref in enumerate(parts)], sems)
    value = None
    for k, copy in enumerate(copies):
        copy.wait()
        term = buf[k].astype(F32)
        value = term if value is None else value + term
    value = value.astype(BF16).astype(F32)
    keys, values = value[:, :HD], value[:, HD:]
    part = HD // 4
    lane = lax.broadcasted_iota(jnp.int32, keys.shape, 1)
    odd = (lane & part) != 0
    swapped = jnp.where(odd, pltpu.roll(keys, part, 1), pltpu.roll(keys, HD - part, 1))
    out[:, :HD] = (keys * cosine[...] + swapped * sine[...]).astype(BF16)
    out[:, HD:] = values.astype(BF16)


def key_value(parts, cosine, sine):
    shape = (parts[0].shape[0], parts[0].shape[1] // 5)
    return pl.pallas_call(
        functools.partial(key_value_kernel, len(parts)),
        in_specs=[in_vmem()] * 2 + [anywhere()] * len(parts),
        out_specs=in_vmem(),
        out_shape=jax.ShapeDtypeStruct(shape, BF16),
        scratch_shapes=[
            pltpu.VMEM((len(parts), *shape), BF16),
            pltpu.SemaphoreType.DMA((len(parts),)),
        ],
        name="key_value",
    )(cosine, sine, *parts)


def query_kernel(units, cosine, sine, *refs):
    parts, (out, buf, sems) = refs[:units], refs[units:]
    wide = out.shape[1]
    copies = start_copies([(ref.at[:, :wide], buf.at[k]) for k, ref in enumerate(parts)], sems)
    cos, sin = cosine[...], sine[...]
    for copy in copies:
        copy.wait()
    for head in range(wide // HD):
        at = slice(head * HD, (head + 1) * HD)
        query = buf[0, :, at].astype(F32)
        for k in range(1, units):
            query = query + buf[k, :, at].astype(F32)
        query = query.astype(BF16).astype(F32)
        swapped = jnp.concatenate([query[:, HD // 2 :], query[:, : HD // 2]], axis=1)
        out[:, at] = (query * cos + swapped * sin).astype(BF16)


def queries(parts, cosine, sine):
    shape = (parts[0].shape[0], parts[0].shape[1] // 5 * 4)
    return pl.pallas_call(
        functools.partial(query_kernel, len(parts)),
        in_specs=[in_vmem()] * 2 + [anywhere()] * len(parts),
        out_specs=in_vmem(),
        out_shape=jax.ShapeDtypeStruct(shape, BF16),
        scratch_shapes=[
            pltpu.VMEM((len(parts), *shape), BF16),
            pltpu.SemaphoreType.DMA((len(parts),)),
        ],
        name="queries",
    )(cosine, sine, *parts)


def attend_kernel(rows, slot, place, lens, dest, query, own_kv, other_kv, out):
    group, block, side = place[GROUP], place[UNIT] & (BLOCKS - 1), place[SIDE]
    _, short = row_facts(lens, dest, group ^ (block >> 1), group, rows, slot)
    many = (block & 1) == 1
    first = jnp.where(many, short[0][2], slot)
    second = jnp.where(many, first + short[1][2], slot)

    def segment(shape, axis):
        at = lax.broadcasted_iota(jnp.int32, shape, axis)
        return jnp.where(at >= first, 1, 0) + jnp.where(at >= second, 1, 0)

    shape = (slot, slot)
    allowed = jnp.logical_and(
        segment(shape, 0) == segment(shape, 1),
        lax.broadcasted_iota(jnp.int32, shape, 1) <= lax.broadcasted_iota(jnp.int32, shape, 0),
    )
    mine, theirs = own_kv[...].astype(F32), other_kv[...].astype(F32)
    even = jnp.where(side == 0, mine, theirs)
    odd = jnp.where(side == 0, theirs, mine)
    part = HD // 4

    def whole_head(index):
        pieces = []
        for b in range(2):
            at = slice((2 * index + b) * part, (2 * index + b + 1) * part)
            pieces += [even[:, at], odd[:, at]]
        return jnp.concatenate(pieces, axis=1).astype(BF16)

    heads = [whole_head(i) for i in range(4)]
    scale = 1.0 / math.sqrt(HD)
    count = out.shape[1] // HD
    for head in range(count):
        key, value = heads[head // (count // 2)], heads[2 + head // (count // 2)]
        at = slice(head * HD, (head + 1) * HD)
        scores = dot(query[:, at], key, NT) * scale
        scores = jnp.where(allowed, scores, -1e30)
        weights = jnp.exp(scores - jnp.max(scores, axis=1, keepdims=True))
        attention = (weights / jnp.sum(weights, axis=1, keepdims=True)).astype(BF16)
        out[:, at] = dot(attention, value).astype(BF16)


def attend(place, lens, dest, query, own_kv, other_kv, rows, slot):
    return pl.pallas_call(
        functools.partial(attend_kernel, rows, slot),
        in_specs=[in_smem()] * 3 + [in_vmem()] * 3,
        out_specs=in_vmem(),
        out_shape=jax.ShapeDtypeStruct(query.shape, BF16),
        compiler_params=pltpu.CompilerParams(vmem_limit_bytes=VMEM),
        name="attend",
    )(place, lens, dest, query, own_kv, other_kv)


def output_kernel(units, rows, slot, place, lens, dest, *refs):
    weights, contexts = refs[:4], refs[4 : 4 + 2 * units]
    out, context, weight, buf, order, c_sems, w_sems, out_sems = refs[4 + 2 * units :]
    unit, side, quarter, group = place[UNIT], place[SIDE], place[QUARTER], place[GROUP]
    part = weights[0].shape[2]
    own = 4 * part
    half = 2 * slot
    features = weight.shape[3]
    c_copies, w_copies = [], []
    for e, y in enumerate((side, 1 - side)):
        w_copies.append(
            start_copies(
                [
                    (weights[r].at[:, y], weight.at[e, :, aligned((quarter ^ r) * part, part)])
                    for r in range(4)
                ],
                w_sems,
                4 * e,
            )
        )
        pairs = []
        for k in range(units):
            source = unit ^ k
            lanes = aligned((source >> 2) * 4 * own, 4 * own)
            at = aligned((source & 3) * slot, slot)
            pairs.append((contexts[e * units + k], context.at[e, at, lanes]))
        c_copies.append(start_copies(pairs, c_sems, e * units))
    column = lax.broadcasted_iota(jnp.int32, (1, half), 1)
    row = lax.broadcasted_iota(jnp.int32, (half, half), 0)
    for turn in range(2):
        full, short = row_facts(lens, dest, group ^ turn, group, rows, slot)
        index = column - full[1]
        done = jnp.int32(0)
        for k in range(3):
            inside = jnp.logical_and(column >= short[k][1], column < short[k][1] + short[k][2])
            index = jnp.where(inside, slot + done + column - short[k][1], index)
            done = done + short[k][2]
        order[turn] = jnp.where(row == index, 1.0, 0.0).astype(BF16)
    sums = [None, None]
    sent = []
    for e in range(2):
        for copy in w_copies[e] + c_copies[e]:
            copy.wait()
        for turn in range(2):
            term = dot(
                context[e, turn * half : (turn + 1) * half],
                weight[e].reshape(units * own, features),
            )
            sums[turn] = term if e == 0 else sums[turn] + term
            if e:
                buf[turn] = dot(sums[turn].astype(BF16), order[turn], TN).astype(BF16)
                columns = aligned((group ^ turn) * half, half)
                sent += start_copies([(buf.at[turn], out.at[:, columns])], out_sems, turn)
    for copy in sent:
        copy.wait()


def output(place, lens, dest, weights, contexts, rows, slot):
    units, _, part, features = weights[0].shape
    tokens = BLOCKS * slot
    return pl.pallas_call(
        functools.partial(output_kernel, units, rows, slot),
        in_specs=[in_smem()] * 3 + [anywhere()] * (4 + len(contexts)),
        out_specs=anywhere(),
        out_shape=jax.ShapeDtypeStruct((features, tokens), BF16),
        scratch_shapes=[
            pltpu.VMEM((2, tokens, units * 4 * part), BF16),
            pltpu.VMEM((2, units, 4 * part, features), BF16),
            pltpu.VMEM((2, features, tokens // 2), BF16),
            pltpu.VMEM((2, tokens // 2, tokens // 2), BF16),
            pltpu.SemaphoreType.DMA((len(contexts),)),
            pltpu.SemaphoreType.DMA((8,)),
            pltpu.SemaphoreType.DMA((2,)),
        ],
        compiler_params=pltpu.CompilerParams(vmem_limit_bytes=VMEM),
        name="output",
    )(place, lens, dest, *weights, *contexts)


def swap(value, axis, mask=1):
    size = lax.axis_size(axis)
    return lax.ppermute(value, axis, [(i, i ^ mask) for i in range(size)])


def over_units(values):
    return [values[0]] + [swap(values[k], "tensor", 2 * k) for k in range(1, len(values))]


def all_quarters(value):
    across = swap(value, "parts")
    return [value, swap(value, "dp"), across, swap(across, "dp")]


def body(
    home,
    gain,
    q_values,
    q_scales,
    k_values,
    k_scales,
    v_values,
    v_scales,
    o_values,
    o_scales,
    row_lengths,
    row_dest,
):
    ranks = lax.axis_size("tensor")
    units = ranks // 2
    rank = lax.axis_index("tensor")
    unit, side = rank >> 1, rank & 1
    group = lax.axis_index("dp")
    quarter = (lax.axis_index("parts") & 1) * 2 + group
    features = home.shape[0]
    rows = row_lengths.shape[0] // 2
    slot = home.shape[1] // rows
    kv_head = rank * k_values.shape[0] // HD
    place = jnp.stack([jnp.asarray(v, jnp.int32) for v in (group, unit, side, quarter, kv_head)])

    pieces, o_pieces = weight_pieces(
        place,
        q_values,
        q_scales,
        k_values,
        k_scales,
        v_values,
        v_scales,
        o_values,
        o_scales,
        ranks,
    )
    keep, send, pos = deal(place, row_lengths, row_dest, home, rows, slot, pieces[:1])
    own_gain = lax.dynamic_slice_in_dim(
        gain.astype(F32), unit * 2 * features, 2 * features
    ).reshape(1, -1)
    frequency = rope_base ** (-2.0 * jnp.arange(HD // 2, dtype=F32) / HD)
    phases = pos[:, :1] * frequency[None, :]
    cosine, sine = jnp.cos(phases), jnp.sin(phases)
    part = HD // 4
    own_cos = lax.dynamic_slice_in_dim(cosine, side * part, part, 1)
    own_sin = lax.dynamic_slice_in_dim(sine, side * part, part, 1)
    own_cos = jnp.concatenate([own_cos] * 4, axis=1)
    own_sin = jnp.concatenate([-own_sin, own_sin] * 2, axis=1)
    wide_cos = jnp.concatenate([cosine, cosine], axis=1)
    wide_sin = jnp.concatenate([-sine, sine], axis=1)

    got = swap(send, "dp")
    keep2 = swap(keep, "tensor")
    got2 = lax.ppermute(
        send, ("dp", "tensor"), [(i, i ^ (ranks + 1)) for i in range(2 * ranks)]
    )
    own_piece, *pieces = over_units(pieces)
    own_pieces = [own_piece, swap(own_piece, "dp"), swap(own_piece, "parts")]
    collected, squares = collect(
        [keep, got, keep2, got2],
        pieces,
        [own_gain, own_cos, own_sin, wide_cos, wide_sin, *own_pieces[1:]],
    )

    squares = over_units([squares] * units)
    own_pieces.append(swap(own_pieces[2], "dp"))
    weights = [collected, swap(collected, "dp"), swap(collected, "parts")]
    (o_pieces,) = gate([o_pieces], squares[1:])
    o_moved = lax.all_to_all(o_pieces, "tensor", split_axis=0, concat_axis=0, tiled=True)
    (weights[2],) = gate(weights[2:], [weights[1], own_pieces[3]])

    weights.append(swap(weights[2], "dp"))
    normed = normalize(place, squares, own_gain, keep, got, keep2, got2)
    parts = over_units(project(place, normed, own_pieces, weights, units))
    (o_moved,) = gate([o_moved], parts[:1])
    own_kv = key_value(parts, own_cos, own_sin)
    other_kv = swap(own_kv, "tensor")
    query = queries(parts, wide_cos, wide_sin)
    o_weights = [
        value.reshape(units, 2, *value.shape[1:]) for value in all_quarters(o_moved)
    ]
    context = attend(place, row_lengths, row_dest, query, own_kv, other_kv, rows, slot)
    mine = [context]
    for k in range(1, units):
        mine.append(swap(mine[k & (k - 1)], "tensor", 2 * (k & -k)))
    theirs = [swap(value, "tensor") for value in mine]
    return output(place, row_lengths, row_dest, o_weights, mine + theirs, rows, slot)


def solution(mesh):
    in_specs = (
        P("tensor", ("parts", "dp")),
        P(),
        P(None, "tensor"),
        P(None, "tensor"),
        P("tensor", None),
        P(),
        P("tensor", None),
        P(),
        P("tensor", None),
        P("tensor", None),
        P("parts"),
        P("parts"),
    )
    out_specs = P("tensor", ("parts", "dp"))
    return jax.shard_map(body, mesh=mesh, in_specs=in_specs, out_specs=out_specs, check_vma=False)
```

```python
import functools
import math

import jax
import jax.numpy as jnp
from jax import lax
from jax.experimental import pallas as pl
from jax.experimental.pallas import tpu as pltpu
from jax.sharding import PartitionSpec as P

D = 8192
HD = 128
BLOCKS = 4

epsilon = 1e-06
rope_base = 1000000.0

F32 = jnp.float32
BF16 = jnp.bfloat16
NN = (((1,), (0,)), ((), ()))
NT = (((1,), (1,)), ((), ()))
TN = (((0,), (0,)), ((), ()))
VMEM = 40 << 20
ALL = 60 << 20


def dot(a, b, dims=NN):
    return lax.dot_general(a, b, dims, preferred_element_type=F32)


def in_vmem():
    return pl.BlockSpec(memory_space=pltpu.VMEM)


def in_smem():
    return pl.BlockSpec(memory_space=pltpu.SMEM)


def anywhere():
    return pl.BlockSpec(memory_space=pl.ANY)


def in_hbm():
    return pl.BlockSpec(memory_space=pltpu.HBM)


def start_copies(pairs, sems, first=0):
    copies = [
        pltpu.make_async_copy(source, target, sems.at[first + i])
        for i, (source, target) in enumerate(pairs)
    ]
    for copy in copies:
        copy.start()
    return copies


def aligned(value, size):
    return pl.ds(pl.multiple_of(value, size), size)


GROUP, UNIT, SIDE, QUARTER, KV_HEAD = range(5)


def row_facts(lens, dest, source, target, rows, slot):
    zero = jnp.int32(0)
    start, seen = zero, zero
    full = [zero, zero]
    short = [[zero, zero, zero] for _ in range(3)]
    for i in range(rows):
        mine = dest[source * rows + i] == target
        size = jnp.where(mine, lens[source * rows + i], 0)
        is_full = size == slot
        is_short = jnp.logical_and(mine, size != slot)
        full = [jnp.where(is_full, i, full[0]), jnp.where(is_full, start, full[1])]
        for k in range(3):
            hit = jnp.logical_and(is_short, seen == k)
            for e, value in enumerate((jnp.int32(i), start, size)):
                short[k][e] = jnp.where(hit, value, short[k][e])
        seen = seen + jnp.where(is_short, 1, 0)
        start = start + size
    return full, short


def pieces_kernel(units, count, place, qs, ks, vs, os, q_hbm, k_hbm, v_hbm, o_hbm, *rest):
    rest = rest[count:]
    outs, o_out = rest[:units], rest[units]
    q_buf, k_buf, v_buf, o_buf, pieces, o_pieces, in_sems, out_sems = rest[units + 1 :]
    unit, quarter, head = place[UNIT], place[QUARTER], place[KV_HEAD]
    _, size, own = q_buf.shape
    part = k_buf.shape[1]
    width = min(size, own)
    ranks, o_rows, features = o_pieces.shape
    copies = []
    for k in range(units):
        at = ((unit ^ k) * 4 + quarter) * size
        copies.append(
            start_copies(
                [
                    (q_hbm.at[aligned(at, size)], q_buf.at[k]),
                    (k_hbm.at[:, aligned(at, size)], k_buf.at[k]),
                    (v_hbm.at[:, aligned(at, size)], v_buf.at[k]),
                ],
                in_sems,
                3 * k,
            )
        )
    (o_copy,) = start_copies(
        [(o_hbm.at[aligned(quarter * o_rows, o_rows)], o_buf)], in_sems, 3 * units
    )
    sent = []
    for k in range(units):
        for copy in copies[k]:
            copy.wait()
        base = ((unit ^ k) * 4 + quarter) * (size // HD)
        for i in range(size // HD):
            rows = slice(i * HD, (i + 1) * HD)
            for h in range(own // HD):
                cols = slice(h * HD, (h + 1) * HD)
                scaled = q_buf[k, rows, cols].astype(F32) * qs[h, base + i]
                pieces[k, rows, cols] = scaled.astype(BF16)
            turn, lane = divmod(i * HD, width)
            at = size + 2 * part * turn
            lanes = slice(lane, lane + HD)
            pieces[k, at : at + part, lanes] = (
                k_buf[k, :, rows].astype(F32) * ks[head, base + i]
            ).astype(BF16)
            pieces[k, at + part : at + 2 * part, lanes] = (
                v_buf[k, :, rows].astype(F32) * vs[head, base + i]
            ).astype(BF16)
        if width < own:
            pieces[k, size:, width:] = jnp.zeros((2 * part, own - width), BF16)
        sent += start_copies([(pieces.at[k], outs[k])], out_sems, k)
    o_copy.wait()
    o_head = quarter * o_rows // HD
    for rank in range(ranks):
        for i in range(features // HD):
            block = rank * (features // HD) + i
            scaled = o_buf[:, block * HD : (block + 1) * HD].astype(F32) * os[o_head, block]
            o_pieces[rank, :, i * HD : (i + 1) * HD] = scaled.astype(BF16)
    sent += start_copies([(o_pieces, o_out)], out_sems, units)
    for copy in sent:
        copy.wait()


def weight_pieces(
    place,
    q_values,
    q_scales,
    k_values,
    k_scales,
    v_values,
    v_scales,
    o_values,
    o_scales,
    ranks,
    after,
):
    units = ranks // 2
    o_shape = (ranks, o_values.shape[0] // 4, o_values.shape[1] // ranks)
    own = q_values.shape[1]
    part = k_values.shape[0]
    size = q_values.shape[0] // units // 4
    rows = size + 2 * part * max(1, size // own)
    outs = pl.pallas_call(
        functools.partial(pieces_kernel, units, len(after)),
        in_specs=[in_smem()] * 5 + [in_hbm()] * 4 + [anywhere()] * len(after),
        out_specs=[anywhere()] * (units + 1),
        out_shape=[jax.ShapeDtypeStruct((rows, own), BF16)] * units
        + [jax.ShapeDtypeStruct(o_shape, BF16)],
        scratch_shapes=[
            pltpu.VMEM((units, size, own), BF16),
            pltpu.VMEM((units, part, size), BF16),
            pltpu.VMEM((units, part, size), BF16),
            pltpu.VMEM((o_shape[1], o_values.shape[1]), BF16),
            pltpu.VMEM((units, rows, own), BF16),
            pltpu.VMEM(o_shape, BF16),
            pltpu.SemaphoreType.DMA((3 * units + 1,)),
            pltpu.SemaphoreType.DMA((units + 1,)),
        ],
        compiler_params=pltpu.CompilerParams(vmem_limit_bytes=ALL),
        name="weight_pieces",
    )(
        place,
        q_scales.T,
        k_scales,
        v_scales,
        o_scales,
        q_values,
        k_values,
        v_values,
        o_values,
        *after,
    )
    return outs[:units], outs[units]


def deal_kernel(rows, slot, place, lens, dest, home, keep, send, pos, pick):
    step = pl.program_id(0)
    group, block = place[GROUP], place[UNIT] & (BLOCKS - 1)

    @pl.when(step == 0)
    def _():
        column = lax.broadcasted_iota(jnp.int32, (slot, 1), 0)
        lane = lax.broadcasted_iota(jnp.int32, (slot, rows * slot), 1)
        for turn in range(2):
            full, short = row_facts(lens, dest, group, group ^ turn, rows, slot)
            first = short[0][2]
            second = first + short[1][2]
            from_short = jnp.where(
                column < first,
                short[0][0] * slot + column,
                jnp.where(
                    column < second,
                    short[1][0] * slot + column - first,
                    short[2][0] * slot + column - second,
                ),
            )
            for kind, index in enumerate((full[0] * slot + column, from_short)):
                at = (turn * 2 + kind) * slot
                pick[at : at + slot, :] = jnp.where(lane == index, 1.0, 0.0).astype(BF16)
        _, short = row_facts(lens, dest, group ^ (block >> 1), group, rows, slot)
        first = short[0][2]
        second = first + short[1][2]
        begin = jnp.where(column < first, 0, jnp.where(column < second, first, second))
        place_in_row = column - jnp.where((block & 1) == 1, begin, 0)
        pos[...] = jnp.broadcast_to(place_in_row.astype(F32), pos.shape)

    taken = dot(pick[...], home[...], NT)
    half = 2 * slot
    keep[...] = taken[:half].astype(BF16)
    send[...] = taken[half:].astype(BF16)


def deal(place, lens, dest, home, rows, slot):
    features = home.shape[0]
    width = min(features, 256)
    tokens = BLOCKS * slot
    return pl.pallas_call(
        functools.partial(deal_kernel, rows, slot),
        grid=(features // width,),
        in_specs=[
            in_smem(),
            in_smem(),
            in_smem(),
            pl.BlockSpec((width, home.shape[1]), lambda i: (i, 0)),
        ],
        out_specs=[
            pl.BlockSpec((tokens // 2, width), lambda i: (0, i)),
            pl.BlockSpec((tokens // 2, width), lambda i: (0, i)),
            pl.BlockSpec((slot, 128), lambda i: (0, 0)),
        ],
        out_shape=[
            jax.ShapeDtypeStruct((tokens // 2, features), BF16),
            jax.ShapeDtypeStruct((tokens // 2, features), BF16),
            jax.ShapeDtypeStruct((slot, 128), F32),
        ],
        scratch_shapes=[
            pltpu.VMEM((tokens, rows * slot), BF16),
        ],
        compiler_params=pltpu.CompilerParams(vmem_limit_bytes=ALL),
        name="deal",
    )(place, lens, dest, home)


def collect_kernel(count, extra, *refs):
    tokens, pieces = refs[:4], refs[4 : 4 + count]
    out, sums = refs[4 + count + extra : 6 + count + extra]
    x_buf, buf, x_sems, sems, out_sems = refs[-5:]
    copies = start_copies([(ref, buf.at[k]) for k, ref in enumerate(pieces)], sems)
    x_copies = start_copies([(ref, x_buf.at[i]) for i, ref in enumerate(tokens)], x_sems)
    sent = []
    for k, copy in enumerate(copies):
        copy.wait()
        sent += start_copies([(buf.at[k], out.at[k])], out_sems, k)
    _, half, features = x_buf.shape
    for i in range(2):
        total = None
        for j in (i, i + 2):
            x_copies[j].wait()
            for at in range(features // 128):
                piece = x_buf[j, :, at * 128 : (at + 1) * 128].astype(F32)
                total = piece * piece if total is None else total + piece * piece
        sums[:, i * half : (i + 1) * half] = jnp.broadcast_to(
            jnp.sum(total.T, axis=0, keepdims=True), (8, half)
        )
    for copy in sent:
        copy.wait()


def collect(tokens, pieces, after):
    count = len(pieces)
    half, features = tokens[0].shape
    return pl.pallas_call(
        functools.partial(collect_kernel, count, len(after)),
        in_specs=[anywhere()] * (4 + count + len(after)),
        out_specs=[anywhere(), in_vmem()],
        out_shape=[
            jax.ShapeDtypeStruct((count, *pieces[0].shape), BF16),
            jax.ShapeDtypeStruct((8, 2 * half), F32),
        ],
        scratch_shapes=[
            pltpu.VMEM((4, half, features), BF16),
            pltpu.VMEM((count, *pieces[0].shape), BF16),
            pltpu.SemaphoreType.DMA((4,)),
            pltpu.SemaphoreType.DMA((count,)),
            pltpu.SemaphoreType.DMA((count,)),
        ],
        compiler_params=pltpu.CompilerParams(vmem_limit_bytes=VMEM),
        name="collect",
    )(*tokens, *pieces, *after)


def gate_kernel(*refs):
    pass


def gate(through, after):
    count = len(through)
    return pl.pallas_call(
        gate_kernel,
        in_specs=[anywhere()] * (count + len(after)),
        out_specs=[anywhere()] * count,
        out_shape=[jax.ShapeDtypeStruct(value.shape, value.dtype) for value in through],
        input_output_aliases={i: i for i in range(count)},
        compiler_params=pltpu.CompilerParams(vmem_limit_bytes=VMEM),
        name="gate",
    )(*through, *after)


def normalize_kernel(units, place, *rest):
    squares, (gain, keep, got, keep2, got2) = rest[:units], rest[units : units + 5]
    out, x_buf, normed, x_sems, out_sems = rest[units + 5 :]
    side = place[SIDE]
    _, half, features = x_buf.shape
    copies = start_copies(
        [(ref, x_buf.at[i]) for i, ref in enumerate((keep, got, keep2, got2))], x_sems
    )
    total = squares[0][...]
    for ref in squares[1:]:
        total = total + ref[...]
    inverse = lax.rsqrt(total / D + epsilon).T[:, :1]
    sent = []
    for i in range(4):
        at = side if i < 2 else 1 - side
        lanes = aligned(at * features, features)
        rows = slice((i & 1) * half, ((i & 1) + 1) * half)
        copies[i].wait()
        wide_rows = x_buf[i].astype(F32)
        normed[i] = (wide_rows * inverse[rows] * gain[:, lanes]).astype(BF16)
        sent += start_copies([(normed.at[i], out.at[rows, lanes])], out_sems, i)
    for copy in sent:
        copy.wait()


def normalize(place, squares, gain, keep, got, keep2, got2):
    half, features = keep.shape
    return pl.pallas_call(
        functools.partial(normalize_kernel, len(squares)),
        in_specs=[in_smem()] + [in_vmem()] * (len(squares) + 1) + [anywhere()] * 4,
        out_specs=anywhere(),
        out_shape=jax.ShapeDtypeStruct((2 * half, 2 * features), BF16),
        scratch_shapes=[
            pltpu.VMEM((4, half, features), BF16),
            pltpu.VMEM((4, half, features), BF16),
            pltpu.SemaphoreType.DMA((4,)),
            pltpu.SemaphoreType.DMA((4,)),
        ],
        compiler_params=pltpu.CompilerParams(vmem_limit_bytes=VMEM),
        name="normalize",
    )(place, *squares, gain, keep, got, keep2, got2)


def project_kernel(units, place, normed, *rest):
    own_pieces, weights, outs = rest[:4], rest[4:8], rest[8:12]
    weight, tokens, buf, x_sem, w_sems, out_sems = rest[12:]
    unit, quarter = place[UNIT], place[QUARTER]
    count, wide = tokens.shape
    slot = count // BLOCKS
    own = weight.shape[3]
    size = wide // 4
    width = min(size, own)
    part = (weight.shape[2] - size) // (size // width)
    (x_copy,) = start_copies([(normed, tokens)], x_sem)
    copies = start_copies(
        [
            (
                weights[r].at[k - 1] if k else own_pieces[r],
                weight.at[quarter ^ r, (k >> 2) * 4 + ((unit ^ k) & 3)],
            )
            for k in range(units)
            for r in range(4)
        ],
        w_sems,
    )
    x_copy.wait()
    sent = []

    def hand_out(group, cols, index, chunk, place_in_chunk):
        for k in range(4 * group, 4 * group + 4):
            rows = aligned(((unit ^ k) & 3) * slot, slot)
            target = outs[2 * chunk + (k & 1)].at[k >> 1, :, place_in_chunk]
            sent.extend(start_copies([(buf.at[group, rows, cols], target)], out_sems, 5 * k + index))

    for group in range(units // BLOCKS):
        sources = slice(group * 4, group * 4 + 4)
        if group == 0:
            for copy in copies:
                copy.wait()
        value = None
        for q in range(4):
            for e in range(size // width):
                at = q * size + e * width
                first = size + e * part
                middle, last = first + part // 2, first + part
                w = jnp.concatenate(
                    [
                        weight[q, sources, first:middle, :width].reshape(2 * part, width),
                        weight[q, sources, middle:last, :width].reshape(2 * part, width),
                    ],
                    axis=0,
                )
                term = dot(tokens[:, at : at + width], w, NT)
                value = term if value is None else value + term
        cols = slice(4 * own, 4 * own + 4 * part)
        buf[group, :, cols] = value.astype(BF16)
        hand_out(group, cols, 4, 0, slice(2 * own, 2 * own + 4 * part))
        for s in range(4):
            value = None
            for q in range(4):
                term = dot(tokens[:, q * size : (q + 1) * size], weight[q, group * 4 + s, :size])
                value = term if value is None else value + term
            cols = slice(s * own, (s + 1) * own)
            buf[group, :, cols] = value.astype(BF16)
            hand_out(group, cols, s, s >> 1, slice((s & 1) * own, ((s & 1) + 1) * own))
    for copy in sent:
        copy.wait()


def project(place, normed, own_pieces, weights, units):
    tokens, wide = normed.shape
    slot = tokens // BLOCKS
    rows, own = own_pieces[0].shape
    size = wide // 4
    part = (rows - size) // (size // min(size, own))
    groups = units // BLOCKS
    outs = pl.pallas_call(
        functools.partial(project_kernel, units),
        in_specs=[in_smem()] + [anywhere()] * 9,
        out_specs=[anywhere()] * 4,
        out_shape=[jax.ShapeDtypeStruct((units // 2, slot, 2 * own + 4 * part), BF16)] * 2
        + [jax.ShapeDtypeStruct((units // 2, slot, 2 * own), BF16)] * 2,
        scratch_shapes=[
            pltpu.VMEM((4, units, rows, own), BF16),
            pltpu.VMEM((tokens, wide), BF16),
            pltpu.VMEM((groups, tokens, 4 * own + 4 * part), BF16),
            pltpu.SemaphoreType.DMA((1,)),
            pltpu.SemaphoreType.DMA((4 * units,)),
            pltpu.SemaphoreType.DMA((5 * units,)),
        ],
        compiler_params=pltpu.CompilerParams(vmem_limit_bytes=ALL),
        name="project",
    )(place, normed, *own_pieces, *weights)
    return outs


def pair_sum_kernel(kept, got, *outs):
    for i, out in enumerate(outs):
        out[...] = (kept[i + 1].astype(F32) + got[i + 1].astype(F32)).astype(BF16)


def pair_sums(kept, got):
    count = kept.shape[0] - 1
    return pl.pallas_call(
        pair_sum_kernel,
        in_specs=[in_vmem()] * 2,
        out_specs=[in_vmem()] * count,
        out_shape=[jax.ShapeDtypeStruct(kept.shape[1:], BF16)] * count,
        compiler_params=pltpu.CompilerParams(vmem_limit_bytes=VMEM),
        name="pair_sums",
    )(kept, got)


def all_parts(refs, cols):
    kept, got = refs[:2]
    value = kept[0, :, cols].astype(F32) + got[0, :, cols].astype(F32)
    for ref in refs[2:]:
        value = value + ref[:, cols].astype(F32)
    return value.astype(BF16).astype(F32)


def key_value_kernel(cosine, sine, *refs):
    parts, out = refs[:-1], refs[-1]
    wide = parts[0].shape[2]
    value = all_parts(parts, slice(wide - out.shape[1], wide))
    keys, values = value[:, :HD], value[:, HD:]
    part = HD // 4
    lane = lax.broadcasted_iota(jnp.int32, keys.shape, 1)
    odd = (lane & part) != 0
    swapped = jnp.where(odd, pltpu.roll(keys, part, 1), pltpu.roll(keys, HD - part, 1))
    out[:, :HD] = (keys * cosine[...] + swapped * sine[...]).astype(BF16)
    out[:, HD:] = values.astype(BF16)


def key_value(parts, cosine, sine):
    return pl.pallas_call(
        key_value_kernel,
        in_specs=[in_vmem()] * (2 + len(parts)),
        out_specs=in_vmem(),
        out_shape=jax.ShapeDtypeStruct((parts[0].shape[1], parts[0].shape[2] // 3), BF16),
        compiler_params=pltpu.CompilerParams(vmem_limit_bytes=VMEM),
        name="key_value",
    )(cosine, sine, *parts)


def query_kernel(count, cosine, sine, *refs):
    parts, out = refs[:count], refs[-1]
    cos, sin = cosine[...], sine[...]
    for head in range(out.shape[1] // HD):
        at = slice(head * HD, (head + 1) * HD)
        query = all_parts(parts, at)
        out[:, at] = (query * cos + pltpu.roll(query, HD // 2, 1) * sin).astype(BF16)


def queries(parts, cosine, sine, wide, after):
    return pl.pallas_call(
        functools.partial(query_kernel, len(parts)),
        in_specs=[in_vmem()] * (2 + len(parts)) + [anywhere()] * len(after),
        out_specs=in_vmem(),
        out_shape=jax.ShapeDtypeStruct((parts[0].shape[1], wide), BF16),
        compiler_params=pltpu.CompilerParams(vmem_limit_bytes=VMEM),
        name="queries",
    )(cosine, sine, *parts, *after)


def attend_kernel(kv_head, rows, slot, place, lens, dest, query, own_kv, other_kv, out):
    group, block, side = place[GROUP], place[UNIT] & (BLOCKS - 1), place[SIDE]
    _, short = row_facts(lens, dest, group ^ (block >> 1), group, rows, slot)
    many = (block & 1) == 1
    first = jnp.where(many, short[0][2], slot)
    second = jnp.where(many, first + short[1][2], slot)

    def segment(shape, axis):
        at = lax.broadcasted_iota(jnp.int32, shape, axis)
        return jnp.where(at >= first, 1, 0) + jnp.where(at >= second, 1, 0)

    shape = (slot, slot)
    allowed = jnp.logical_and(
        segment(shape, 0) == segment(shape, 1),
        lax.broadcasted_iota(jnp.int32, shape, 1) <= lax.broadcasted_iota(jnp.int32, shape, 0),
    )
    mine, theirs = own_kv[...].astype(F32), other_kv[...].astype(F32)
    even = jnp.where(side == 0, mine, theirs)
    odd = jnp.where(side == 0, theirs, mine)
    part = HD // 4

    def whole_head(index):
        pieces = []
        for b in range(2):
            at = slice((2 * index + b) * part, (2 * index + b + 1) * part)
            pieces += [even[:, at], odd[:, at]]
        return jnp.concatenate(pieces, axis=1).astype(BF16)

    key, value = whole_head(kv_head), whole_head(2 + kv_head)
    scale = 1.0 / math.sqrt(HD)
    for head in range(out.shape[1] // HD):
        at = slice(head * HD, (head + 1) * HD)
        scores = dot(query[:, at], key, NT) * scale
        scores = jnp.where(allowed, scores, -1e30)
        weights = jnp.exp(scores - jnp.max(scores, axis=1, keepdims=True))
        attention = (weights / jnp.sum(weights, axis=1, keepdims=True)).astype(BF16)
        out[:, at] = dot(attention, value).astype(BF16)


def attend(place, lens, dest, query, own_kv, other_kv, kv_head, rows, slot):
    return pl.pallas_call(
        functools.partial(attend_kernel, kv_head, rows, slot),
        in_specs=[in_smem()] * 3 + [in_vmem()] * 3,
        out_specs=in_vmem(),
        out_shape=jax.ShapeDtypeStruct(query.shape, BF16),
        compiler_params=pltpu.CompilerParams(vmem_limit_bytes=VMEM),
        name="attend",
    )(place, lens, dest, query, own_kv, other_kv)


def output_kernel(units, rows, slot, place, lens, dest, *refs):
    weights, contexts = refs[:4], refs[4 : 4 + 4 * units]
    out, context, weight, buf, order, c_sems, w_sems, out_sems = refs[4 + 4 * units :]
    unit, side, quarter, group = place[UNIT], place[SIDE], place[QUARTER], place[GROUP]
    part = weights[0].shape[2]
    own = 4 * part
    half = 2 * slot
    features = weight.shape[3]
    c_copies, w_copies = [], []
    for e, y in enumerate((side, 1 - side)):
        w_copies.append(
            start_copies(
                [
                    (weights[r].at[:, y], weight.at[e, :, aligned((quarter ^ r) * part, part)])
                    for r in range(4)
                ],
                w_sems,
                4 * e,
            )
        )
        pairs = []
        for k in range(units):
            source = unit ^ k
            at = aligned((source & 3) * slot, slot)
            for h in range(2):
                lanes = aligned((source >> 2) * 4 * own + h * 2 * own, 2 * own)
                pairs.append((contexts[(2 * h + e) * units + k], context.at[e, at, lanes]))
        c_copies.append(start_copies(pairs, c_sems, e * 2 * units))
    column = lax.broadcasted_iota(jnp.int32, (1, half), 1)
    row = lax.broadcasted_iota(jnp.int32, (half, half), 0)
    for turn in range(2):
        full, short = row_facts(lens, dest, group ^ turn, group, rows, slot)
        index = column - full[1]
        done = jnp.int32(0)
        for k in range(3):
            inside = jnp.logical_and(column >= short[k][1], column < short[k][1] + short[k][2])
            index = jnp.where(inside, slot + done + column - short[k][1], index)
            done = done + short[k][2]
        order[turn] = jnp.where(row == index, 1.0, 0.0).astype(BF16)
    sums = [None, None]
    sent = []
    for e in range(2):
        for copy in w_copies[e] + c_copies[e]:
            copy.wait()
        for turn in range(2):
            term = dot(
                context[e, turn * half : (turn + 1) * half],
                weight[e].reshape(units * own, features),
            )
            sums[turn] = term if e == 0 else sums[turn] + term
            if e:
                buf[turn] = dot(sums[turn].astype(BF16), order[turn], TN).astype(BF16)
                columns = aligned((group ^ turn) * half, half)
                sent += start_copies([(buf.at[turn], out.at[:, columns])], out_sems, turn)
    for copy in sent:
        copy.wait()


def output(place, lens, dest, weights, contexts, rows, slot):
    units, _, part, features = weights[0].shape
    tokens = BLOCKS * slot
    return pl.pallas_call(
        functools.partial(output_kernel, units, rows, slot),
        in_specs=[in_smem()] * 3 + [anywhere()] * (4 + len(contexts)),
        out_specs=anywhere(),
        out_shape=jax.ShapeDtypeStruct((features, tokens), BF16),
        scratch_shapes=[
            pltpu.VMEM((2, tokens, units * 4 * part), BF16),
            pltpu.VMEM((2, units, 4 * part, features), BF16),
            pltpu.VMEM((2, features, tokens // 2), BF16),
            pltpu.VMEM((2, tokens // 2, tokens // 2), BF16),
            pltpu.SemaphoreType.DMA((len(contexts),)),
            pltpu.SemaphoreType.DMA((8,)),
            pltpu.SemaphoreType.DMA((2,)),
        ],
        compiler_params=pltpu.CompilerParams(vmem_limit_bytes=VMEM),
        name="output",
    )(place, lens, dest, *weights, *contexts)


def swap(value, axis, mask=1):
    size = lax.axis_size(axis)
    return lax.ppermute(value, axis, [(i, i ^ mask) for i in range(size)])


def over_units(values):
    return [values[0]] + [swap(values[k], "tensor", 2 * k) for k in range(1, len(values))]


def all_quarters(value):
    across = swap(value, "parts")
    return [value, swap(value, "dp"), across, swap(across, "dp")]


def body(
    home,
    gain,
    q_values,
    q_scales,
    k_values,
    k_scales,
    v_values,
    v_scales,
    o_values,
    o_scales,
    row_lengths,
    row_dest,
):
    ranks = lax.axis_size("tensor")
    units = ranks // 2
    rank = lax.axis_index("tensor")
    unit, side = rank >> 1, rank & 1
    group = lax.axis_index("dp")
    quarter = (lax.axis_index("parts") & 1) * 2 + group
    features = home.shape[0]
    rows = row_lengths.shape[0] // 2
    slot = home.shape[1] // rows
    kv_head = rank * k_values.shape[0] // HD
    place = jnp.stack([jnp.asarray(v, jnp.int32) for v in (group, unit, side, quarter, kv_head)])

    keep, send, pos = deal(place, row_lengths, row_dest, home, rows, slot)
    pieces, o_pieces = weight_pieces(
        place,
        q_values,
        q_scales,
        k_values,
        k_scales,
        v_values,
        v_scales,
        o_values,
        o_scales,
        ranks,
        [keep],
    )
    own_gain = lax.dynamic_slice_in_dim(
        gain.astype(F32), unit * 2 * features, 2 * features
    ).reshape(1, -1)
    frequency = rope_base ** (-2.0 * jnp.arange(HD // 2, dtype=F32) / HD)
    phases = pos[:, :1] * frequency[None, :]
    cosine, sine = jnp.cos(phases), jnp.sin(phases)
    part = HD // 4
    own_cos = lax.dynamic_slice_in_dim(cosine, side * part, part, 1)
    own_sin = lax.dynamic_slice_in_dim(sine, side * part, part, 1)
    own_cos = jnp.concatenate([own_cos] * 4, axis=1)
    own_sin = jnp.concatenate([-own_sin, own_sin] * 2, axis=1)
    wide_cos = jnp.concatenate([cosine, cosine], axis=1)
    wide_sin = jnp.concatenate([-sine, sine], axis=1)

    got = swap(send, "dp")
    keep2 = swap(keep, "tensor")
    got2 = lax.ppermute(
        send, ("dp", "tensor"), [(i, i ^ (ranks + 1)) for i in range(2 * ranks)]
    )
    own_piece, *pieces = over_units(pieces)
    own_pieces = [own_piece, swap(own_piece, "dp"), swap(own_piece, "parts")]
    collected, squares = collect(
        [keep, got, keep2, got2],
        pieces,
        [own_gain, own_cos, own_sin, wide_cos, wide_sin, *own_pieces[1:]],
    )

    squares = over_units([squares] * units)
    own_pieces.append(swap(own_pieces[2], "dp"))
    weights = [collected, swap(collected, "dp"), swap(collected, "parts")]
    (o_pieces,) = gate([o_pieces], squares[1:])
    o_moved = lax.all_to_all(o_pieces, "tensor", split_axis=0, concat_axis=0, tiled=True)
    normed = normalize(place, squares, own_gain, keep, got, keep2, got2)
    (weights[2],) = gate(weights[2:], [weights[1], own_pieces[3], normed])

    weights.append(swap(weights[2], "dp"))
    kept_a, near_a, kept_b, near_b = project(place, normed, own_pieces, weights, units)
    (o_moved,) = gate([o_moved], [kept_a])
    parts = []
    for kept, near in ((kept_a, near_a), (kept_b, near_b)):
        got = swap(near, "tensor", 2)
        sums = pair_sums(kept, got)
        far = [swap(value, "tensor", 4 * (i + 1)) for i, value in enumerate(sums)]
        parts.append([kept, got, *far])
    own_kv = key_value(parts[0], own_cos, own_sin)
    other_kv = swap(own_kv, "tensor")
    o_weights = [
        value.reshape(units, 2, *value.shape[1:]) for value in all_quarters(o_moved)
    ]
    contexts = []
    for h in range(2):
        query = queries(parts[h], wide_cos, wide_sin, near_b.shape[2], contexts[units : units + 1])
        context = attend(
            place, row_lengths, row_dest, query, own_kv, other_kv, h, rows, slot
        )
        mine, theirs = [context], [swap(context, "tensor")]
        for k in range(1, units):
            mine.append(swap(mine[k & (k - 1)], "tensor", 2 * (k & -k)))
            if k == 2:
                (mine[2],) = gate(mine[2:], [mine[1], theirs[0]])
        theirs += [swap(value, "tensor") for value in mine[1:]]
        contexts += mine + theirs
    return output(place, row_lengths, row_dest, o_weights, contexts, rows, slot)


def solution(mesh):
    in_specs = (
        P("tensor", ("parts", "dp")),
        P(),
        P(None, "tensor"),
        P(None, "tensor"),
        P("tensor", None),
        P(),
        P("tensor", None),
        P(),
        P("tensor", None),
        P("tensor", None),
        P("parts"),
        P("parts"),
    )
    out_specs = P("tensor", ("parts", "dp"))
    return jax.shard_map(body, mesh=mesh, in_specs=in_specs, out_specs=out_specs, check_vma=False)
```

```python
import functools
import math

import jax
import jax.numpy as jnp
from jax import lax
from jax.experimental import pallas as pl
from jax.experimental.pallas import tpu as pltpu
from jax.sharding import PartitionSpec as P

D = 8192
HD = 128
BLOCKS = 4

epsilon = 1e-06
rope_base = 1000000.0

F32 = jnp.float32
BF16 = jnp.bfloat16
NN = (((1,), (0,)), ((), ()))
NT = (((1,), (1,)), ((), ()))
TN = (((0,), (0,)), ((), ()))
VMEM = 40 << 20
ALL = 60 << 20


def dot(a, b, dims=NN):
    return lax.dot_general(a, b, dims, preferred_element_type=F32)


def in_vmem():
    return pl.BlockSpec(memory_space=pltpu.VMEM)


def in_smem():
    return pl.BlockSpec(memory_space=pltpu.SMEM)


def anywhere():
    return pl.BlockSpec(memory_space=pl.ANY)


def in_hbm():
    return pl.BlockSpec(memory_space=pltpu.HBM)


def start_copies(pairs, sems, first=0):
    copies = [
        pltpu.make_async_copy(source, target, sems.at[first + i])
        for i, (source, target) in enumerate(pairs)
    ]
    for copy in copies:
        copy.start()
    return copies


def aligned(value, size):
    return pl.ds(pl.multiple_of(value, size), size)


GROUP, UNIT, SIDE, QUARTER, KV_HEAD = range(5)


def row_facts(lens, dest, source, target, rows, slot):
    zero = jnp.int32(0)
    start, seen = zero, zero
    full = [zero, zero]
    short = [[zero, zero, zero] for _ in range(3)]
    for i in range(rows):
        mine = dest[source * rows + i] == target
        size = jnp.where(mine, lens[source * rows + i], 0)
        is_full = size == slot
        is_short = jnp.logical_and(mine, size != slot)
        full = [jnp.where(is_full, i, full[0]), jnp.where(is_full, start, full[1])]
        for k in range(3):
            hit = jnp.logical_and(is_short, seen == k)
            for e, value in enumerate((jnp.int32(i), start, size)):
                short[k][e] = jnp.where(hit, value, short[k][e])
        seen = seen + jnp.where(is_short, 1, 0)
        start = start + size
    return full, short


def pieces_kernel(units, count, place, qs, ks, vs, q_hbm, k_hbm, v_hbm, *rest):
    rest = rest[count:]
    outs = rest[:units]
    q_buf, k_buf, v_buf, pieces, in_sems, out_sems = rest[units:]
    unit, quarter, head = place[UNIT], place[QUARTER], place[KV_HEAD]
    _, size, own = q_buf.shape
    part = k_buf.shape[1]
    width = min(size, own)
    copies = []
    for k in range(units):
        at = ((unit ^ k) * 4 + quarter) * size
        copies.append(
            start_copies(
                [
                    (q_hbm.at[aligned(at, size)], q_buf.at[k]),
                    (k_hbm.at[:, aligned(at, size)], k_buf.at[k]),
                    (v_hbm.at[:, aligned(at, size)], v_buf.at[k]),
                ],
                in_sems,
                3 * k,
            )
        )
    sent = []
    for k in range(units):
        for copy in copies[k]:
            copy.wait()
        base = ((unit ^ k) * 4 + quarter) * (size // HD)
        for i in range(size // HD):
            rows = slice(i * HD, (i + 1) * HD)
            for h in range(own // HD):
                cols = slice(h * HD, (h + 1) * HD)
                scaled = q_buf[k, rows, cols].astype(F32) * qs[h, base + i]
                pieces[k, rows, cols] = scaled.astype(BF16)
            turn, lane = divmod(i * HD, width)
            at = size + 2 * part * turn
            lanes = slice(lane, lane + HD)
            pieces[k, at : at + part, lanes] = (
                k_buf[k, :, rows].astype(F32) * ks[head, base + i]
            ).astype(BF16)
            pieces[k, at + part : at + 2 * part, lanes] = (
                v_buf[k, :, rows].astype(F32) * vs[head, base + i]
            ).astype(BF16)
        if width < own:
            pieces[k, size:, width:] = jnp.zeros((2 * part, own - width), BF16)
        sent += start_copies([(pieces.at[k], outs[k])], out_sems, k)
    for copy in sent:
        copy.wait()


def weight_pieces(place, q_values, q_scales, k_values, k_scales, v_values, v_scales, units, after):
    own = q_values.shape[1]
    part = k_values.shape[0]
    size = q_values.shape[0] // units // 4
    rows = size + 2 * part * max(1, size // own)
    return pl.pallas_call(
        functools.partial(pieces_kernel, units, len(after)),
        in_specs=[in_smem()] * 4 + [in_hbm()] * 3 + [anywhere()] * len(after),
        out_specs=[anywhere()] * units,
        out_shape=[jax.ShapeDtypeStruct((rows, own), BF16)] * units,
        scratch_shapes=[
            pltpu.VMEM((units, size, own), BF16),
            pltpu.VMEM((units, part, size), BF16),
            pltpu.VMEM((units, part, size), BF16),
            pltpu.VMEM((units, rows, own), BF16),
            pltpu.SemaphoreType.DMA((3 * units,)),
            pltpu.SemaphoreType.DMA((units,)),
        ],
        compiler_params=pltpu.CompilerParams(vmem_limit_bytes=ALL),
        name="weight_pieces",
    )(place, q_scales.T, k_scales, v_scales, q_values, k_values, v_values, *after)


def o_pieces_kernel(count, place, scales, o_hbm, *rest):
    out, o_buf, pieces, sem, out_sem = rest[count:]
    ranks, rows, features = pieces.shape
    first = place[QUARTER] * rows
    (copy,) = start_copies([(o_hbm.at[aligned(first, rows)], o_buf)], sem)
    copy.wait()
    for rank in range(ranks):
        for i in range(features // HD):
            block = rank * (features // HD) + i
            scaled = o_buf[:, block * HD : (block + 1) * HD].astype(F32) * scales[first // HD, block]
            pieces[rank, :, i * HD : (i + 1) * HD] = scaled.astype(BF16)
    (sent,) = start_copies([(pieces, out)], out_sem)
    sent.wait()


def output_pieces(place, o_values, o_scales, ranks, after):
    shape = (ranks, o_values.shape[0] // 4, o_values.shape[1] // ranks)
    return pl.pallas_call(
        functools.partial(o_pieces_kernel, len(after)),
        in_specs=[in_smem()] * 2 + [in_hbm()] + [anywhere()] * len(after),
        out_specs=anywhere(),
        out_shape=jax.ShapeDtypeStruct(shape, BF16),
        scratch_shapes=[
            pltpu.VMEM((shape[1], o_values.shape[1]), BF16),
            pltpu.VMEM(shape, BF16),
            pltpu.SemaphoreType.DMA((1,)),
            pltpu.SemaphoreType.DMA((1,)),
        ],
        compiler_params=pltpu.CompilerParams(vmem_limit_bytes=ALL),
        name="output_pieces",
    )(place, o_scales, o_values, *after)


def deal_kernel(rows, slot, place, lens, dest, home, keep, send, pos, pick):
    step = pl.program_id(0)
    group, block = place[GROUP], place[UNIT] & (BLOCKS - 1)

    @pl.when(step == 0)
    def _():
        column = lax.broadcasted_iota(jnp.int32, (slot, 1), 0)
        lane = lax.broadcasted_iota(jnp.int32, (slot, rows * slot), 1)
        for turn in range(2):
            full, short = row_facts(lens, dest, group, group ^ turn, rows, slot)
            first = short[0][2]
            second = first + short[1][2]
            from_short = jnp.where(
                column < first,
                short[0][0] * slot + column,
                jnp.where(
                    column < second,
                    short[1][0] * slot + column - first,
                    short[2][0] * slot + column - second,
                ),
            )
            for kind, index in enumerate((full[0] * slot + column, from_short)):
                at = (turn * 2 + kind) * slot
                pick[at : at + slot, :] = jnp.where(lane == index, 1.0, 0.0).astype(BF16)
        _, short = row_facts(lens, dest, group ^ (block >> 1), group, rows, slot)
        first = short[0][2]
        second = first + short[1][2]
        begin = jnp.where(column < first, 0, jnp.where(column < second, first, second))
        place_in_row = column - jnp.where((block & 1) == 1, begin, 0)
        pos[...] = jnp.broadcast_to(place_in_row.astype(F32), pos.shape)

    taken = dot(pick[...], home[...], NT)
    half = 2 * slot
    keep[...] = taken[:half].astype(BF16)
    send[...] = taken[half:].astype(BF16)


def deal(place, lens, dest, home, rows, slot):
    features = home.shape[0]
    width = min(features, 256)
    tokens = BLOCKS * slot
    return pl.pallas_call(
        functools.partial(deal_kernel, rows, slot),
        grid=(features // width,),
        in_specs=[
            in_smem(),
            in_smem(),
            in_smem(),
            pl.BlockSpec((width, home.shape[1]), lambda i: (i, 0)),
        ],
        out_specs=[
            pl.BlockSpec((tokens // 2, width), lambda i: (0, i)),
            pl.BlockSpec((tokens // 2, width), lambda i: (0, i)),
            pl.BlockSpec((slot, 128), lambda i: (0, 0)),
        ],
        out_shape=[
            jax.ShapeDtypeStruct((tokens // 2, features), BF16),
            jax.ShapeDtypeStruct((tokens // 2, features), BF16),
            jax.ShapeDtypeStruct((slot, 128), F32),
        ],
        scratch_shapes=[
            pltpu.VMEM((tokens, rows * slot), BF16),
        ],
        compiler_params=pltpu.CompilerParams(vmem_limit_bytes=ALL),
        name="deal",
    )(place, lens, dest, home)


def collect_kernel(count, extra, *refs):
    tokens, pieces = refs[:4], refs[4 : 4 + count]
    out, sums = refs[4 + count + extra : 6 + count + extra]
    x_buf, buf, x_sems, sems, out_sems = refs[-5:]
    copies = start_copies([(ref, buf.at[k]) for k, ref in enumerate(pieces)], sems)
    x_copies = start_copies([(ref, x_buf.at[i]) for i, ref in enumerate(tokens)], x_sems)
    sent = []
    for k, copy in enumerate(copies):
        copy.wait()
        sent += start_copies([(buf.at[k], out.at[k])], out_sems, k)
    _, half, features = x_buf.shape
    for i in range(2):
        total = None
        for j in (i, i + 2):
            x_copies[j].wait()
            for at in range(features // 128):
                piece = x_buf[j, :, at * 128 : (at + 1) * 128].astype(F32)
                total = piece * piece if total is None else total + piece * piece
        sums[:, i * half : (i + 1) * half] = jnp.broadcast_to(
            jnp.sum(total.T, axis=0, keepdims=True), (8, half)
        )
    for copy in sent:
        copy.wait()


def collect(tokens, pieces, after):
    count = len(pieces)
    half, features = tokens[0].shape
    return pl.pallas_call(
        functools.partial(collect_kernel, count, len(after)),
        in_specs=[anywhere()] * (4 + count + len(after)),
        out_specs=[anywhere(), in_vmem()],
        out_shape=[
            jax.ShapeDtypeStruct((count, *pieces[0].shape), BF16),
            jax.ShapeDtypeStruct((8, 2 * half), F32),
        ],
        scratch_shapes=[
            pltpu.VMEM((4, half, features), BF16),
            pltpu.VMEM((count, *pieces[0].shape), BF16),
            pltpu.SemaphoreType.DMA((4,)),
            pltpu.SemaphoreType.DMA((count,)),
            pltpu.SemaphoreType.DMA((count,)),
        ],
        compiler_params=pltpu.CompilerParams(vmem_limit_bytes=VMEM),
        name="collect",
    )(*tokens, *pieces, *after)


def gate_kernel(*refs):
    pass


def gate(through, after):
    count = len(through)
    return pl.pallas_call(
        gate_kernel,
        in_specs=[anywhere()] * (count + len(after)),
        out_specs=[anywhere()] * count,
        out_shape=[jax.ShapeDtypeStruct(value.shape, value.dtype) for value in through],
        input_output_aliases={i: i for i in range(count)},
        compiler_params=pltpu.CompilerParams(vmem_limit_bytes=VMEM),
        name="gate",
    )(*through, *after)


def normalize_kernel(units, place, *rest):
    squares, (gain, keep, got, keep2, got2) = rest[:units], rest[units : units + 5]
    out, x_buf, normed, x_sems, out_sems = rest[units + 5 :]
    side = place[SIDE]
    _, half, features = x_buf.shape
    copies = start_copies(
        [(ref, x_buf.at[i]) for i, ref in enumerate((keep, got, keep2, got2))], x_sems
    )
    total = squares[0][...]
    for ref in squares[1:]:
        total = total + ref[...]
    inverse = lax.rsqrt(total / D + epsilon).T[:, :1]
    sent = []
    for i in range(4):
        at = side if i < 2 else 1 - side
        lanes = aligned(at * features, features)
        rows = slice((i & 1) * half, ((i & 1) + 1) * half)
        copies[i].wait()
        wide_rows = x_buf[i].astype(F32)
        normed[i] = (wide_rows * inverse[rows] * gain[:, lanes]).astype(BF16)
        sent += start_copies([(normed.at[i], out.at[rows, lanes])], out_sems, i)
    for copy in sent:
        copy.wait()


def normalize(place, squares, gain, keep, got, keep2, got2):
    half, features = keep.shape
    return pl.pallas_call(
        functools.partial(normalize_kernel, len(squares)),
        in_specs=[in_smem()] + [in_vmem()] * (len(squares) + 1) + [anywhere()] * 4,
        out_specs=anywhere(),
        out_shape=jax.ShapeDtypeStruct((2 * half, 2 * features), BF16),
        scratch_shapes=[
            pltpu.VMEM((4, half, features), BF16),
            pltpu.VMEM((4, half, features), BF16),
            pltpu.SemaphoreType.DMA((4,)),
            pltpu.SemaphoreType.DMA((4,)),
        ],
        compiler_params=pltpu.CompilerParams(vmem_limit_bytes=VMEM),
        name="normalize",
    )(place, *squares, gain, keep, got, keep2, got2)


def project_kernel(units, place, tokens, *rest):
    own_pieces, weights, outs = rest[:4], rest[4:8], rest[8:12]
    buf, out_sems = rest[12:]
    unit, quarter = place[UNIT], place[QUARTER]
    count, wide = tokens.shape
    slot = count // BLOCKS
    rows, own = own_pieces[0].shape
    size = wide // 4
    width = min(size, own)
    part = (rows - size) // (size // width)

    def weight(k, r, rows, lanes=slice(None)):
        return weights[r][k - 1, rows, lanes] if k else own_pieces[r][rows, lanes]

    def features(r, first, count):
        return tokens[:, aligned((quarter ^ r) * size + first, count)]

    sent = []

    def hand_out(group, cols, index, chunk, place_in_chunk):
        for k in range(4 * group, 4 * group + 4):
            rows = aligned(((unit ^ k) & 3) * slot, slot)
            target = outs[2 * chunk + (k & 1)].at[k >> 1, :, place_in_chunk]
            sent.extend(start_copies([(buf.at[group, rows, cols], target)], out_sems, 3 * k + index))

    for group in range(units // BLOCKS):
        members = range(4 * group, 4 * group + 4)
        for k in members:
            s = (unit ^ k) & 3
            value = None
            for r in range(4):
                term = dot(features(r, 0, size), weight(k, r, slice(0, size)))
                value = term if value is None else value + term
            buf[group, :, aligned(s * own, own)] = value.astype(BF16)
        hand_out(group, slice(0, 2 * own), 0, 0, slice(0, 2 * own))
        hand_out(group, slice(2 * own, 4 * own), 1, 1, slice(0, 2 * own))
        value = None
        for r in range(4):
            for e in range(size // width):
                pieces = []
                for half in range(2):
                    first = size + e * part + half * (part // 2)
                    rows, lanes = slice(first, first + part // 2), slice(0, width)
                    for s in range(4):
                        k = 4 * group + ((unit & 3) ^ s)
                        piece = weights[r][jnp.maximum(k - 1, 0), rows, lanes]
                        if group == 0:
                            piece = jnp.where(k == 0, own_pieces[r][rows, lanes], piece)
                        pieces.append(piece)
                w = jnp.concatenate(pieces, axis=0)
                term = dot(features(r, e * width, width), w, NT)
                value = term if value is None else value + term
        buf[group, :, 4 * own :] = value.astype(BF16)
        cols = slice(4 * own, 4 * own + 4 * part)
        hand_out(group, cols, 2, 0, slice(2 * own, 2 * own + 4 * part))
    for copy in sent:
        copy.wait()


def project(place, normed, own_pieces, weights, units):
    tokens, wide = normed.shape
    slot = tokens // BLOCKS
    rows, own = own_pieces[0].shape
    size = wide // 4
    part = (rows - size) // (size // min(size, own))
    groups = units // BLOCKS
    outs = pl.pallas_call(
        functools.partial(project_kernel, units),
        in_specs=[in_smem()] + [in_vmem()] * 9,
        out_specs=[anywhere()] * 4,
        out_shape=[jax.ShapeDtypeStruct((units // 2, slot, 2 * own + 4 * part), BF16)] * 2
        + [jax.ShapeDtypeStruct((units // 2, slot, 2 * own), BF16)] * 2,
        scratch_shapes=[
            pltpu.VMEM((groups, tokens, 4 * own + 4 * part), BF16),
            pltpu.SemaphoreType.DMA((3 * units,)),
        ],
        compiler_params=pltpu.CompilerParams(vmem_limit_bytes=VMEM),
        name="project",
    )(place, normed, *own_pieces, *weights)
    return outs


def pair_sum_kernel(kept, got, *outs):
    for i, out in enumerate(outs):
        out[...] = (kept[i + 1].astype(F32) + got[i + 1].astype(F32)).astype(BF16)


def pair_sums(kept, got):
    count = kept.shape[0] - 1
    return pl.pallas_call(
        pair_sum_kernel,
        in_specs=[in_vmem()] * 2,
        out_specs=[in_vmem()] * count,
        out_shape=[jax.ShapeDtypeStruct(kept.shape[1:], BF16)] * count,
        compiler_params=pltpu.CompilerParams(vmem_limit_bytes=VMEM),
        name="pair_sums",
    )(kept, got)


def all_parts(refs, cols):
    kept, got = refs[:2]
    value = kept[0, :, cols].astype(F32) + got[0, :, cols].astype(F32)
    for ref in refs[2:]:
        value = value + ref[:, cols].astype(F32)
    return value.astype(BF16).astype(F32)


def key_value_kernel(count, cosine, sine, *refs):
    parts, out = refs[:count], refs[-1]
    wide = parts[0].shape[2]
    value = all_parts(parts, slice(wide - out.shape[1], wide))
    keys, values = value[:, :HD], value[:, HD:]
    part = HD // 4
    lane = lax.broadcasted_iota(jnp.int32, keys.shape, 1)
    odd = (lane & part) != 0
    swapped = jnp.where(odd, pltpu.roll(keys, part, 1), pltpu.roll(keys, HD - part, 1))
    out[:, :HD] = (keys * cosine[...] + swapped * sine[...]).astype(BF16)
    out[:, HD:] = values.astype(BF16)


def key_value(parts, cosine, sine, after):
    return pl.pallas_call(
        functools.partial(key_value_kernel, len(parts)),
        in_specs=[in_vmem()] * (2 + len(parts)) + [anywhere()] * len(after),
        out_specs=in_vmem(),
        out_shape=jax.ShapeDtypeStruct((parts[0].shape[1], parts[0].shape[2] // 3), BF16),
        compiler_params=pltpu.CompilerParams(vmem_limit_bytes=VMEM),
        name="key_value",
    )(cosine, sine, *parts, *after)


def query_kernel(count, cosine, sine, *refs):
    parts, out = refs[:count], refs[-1]
    cos, sin = cosine[...], sine[...]
    for head in range(out.shape[1] // HD):
        at = slice(head * HD, (head + 1) * HD)
        query = all_parts(parts, at)
        out[:, at] = (query * cos + pltpu.roll(query, HD // 2, 1) * sin).astype(BF16)


def queries(parts, cosine, sine, wide, after):
    return pl.pallas_call(
        functools.partial(query_kernel, len(parts)),
        in_specs=[in_vmem()] * (2 + len(parts)) + [anywhere()] * len(after),
        out_specs=in_vmem(),
        out_shape=jax.ShapeDtypeStruct((parts[0].shape[1], wide), BF16),
        compiler_params=pltpu.CompilerParams(vmem_limit_bytes=VMEM),
        name="queries",
    )(cosine, sine, *parts, *after)


def attend_kernel(kv_head, rows, slot, place, lens, dest, query, own_kv, other_kv, out):
    group, block, side = place[GROUP], place[UNIT] & (BLOCKS - 1), place[SIDE]
    _, short = row_facts(lens, dest, group ^ (block >> 1), group, rows, slot)
    many = (block & 1) == 1
    first = jnp.where(many, short[0][2], slot)
    second = jnp.where(many, first + short[1][2], slot)

    def segment(shape, axis):
        at = lax.broadcasted_iota(jnp.int32, shape, axis)
        return jnp.where(at >= first, 1, 0) + jnp.where(at >= second, 1, 0)

    shape = (slot, slot)
    allowed = jnp.logical_and(
        segment(shape, 0) == segment(shape, 1),
        lax.broadcasted_iota(jnp.int32, shape, 1) <= lax.broadcasted_iota(jnp.int32, shape, 0),
    )
    mine, theirs = own_kv[...].astype(F32), other_kv[...].astype(F32)
    even = jnp.where(side == 0, mine, theirs)
    odd = jnp.where(side == 0, theirs, mine)
    part = HD // 4

    def whole_head(index):
        pieces = []
        for b in range(2):
            at = slice((2 * index + b) * part, (2 * index + b + 1) * part)
            pieces += [even[:, at], odd[:, at]]
        return jnp.concatenate(pieces, axis=1).astype(BF16)

    key, value = whole_head(kv_head), whole_head(2 + kv_head)
    scale = 1.0 / math.sqrt(HD)
    for head in range(out.shape[1] // HD):
        at = slice(head * HD, (head + 1) * HD)
        scores = dot(query[:, at], key, NT) * scale
        scores = jnp.where(allowed, scores, -1e30)
        weights = jnp.exp(scores - jnp.max(scores, axis=1, keepdims=True))
        attention = (weights / jnp.sum(weights, axis=1, keepdims=True)).astype(BF16)
        out[:, at] = dot(attention, value).astype(BF16)


def attend(place, lens, dest, query, own_kv, other_kv, kv_head, rows, slot):
    return pl.pallas_call(
        functools.partial(attend_kernel, kv_head, rows, slot),
        in_specs=[in_smem()] * 3 + [in_vmem()] * 3,
        out_specs=in_vmem(),
        out_shape=jax.ShapeDtypeStruct(query.shape, BF16),
        compiler_params=pltpu.CompilerParams(vmem_limit_bytes=VMEM),
        name="attend",
    )(place, lens, dest, query, own_kv, other_kv)


def output_kernel(units, rows, slot, place, lens, dest, *refs):
    weights, contexts = refs[:4], refs[4 : 4 + 4 * units]
    out, context, weight, buf, order, c_sems, w_sems, out_sems = refs[4 + 4 * units :]
    unit, side, quarter, group = place[UNIT], place[SIDE], place[QUARTER], place[GROUP]
    part = weights[0].shape[2]
    own = 4 * part
    half = 2 * slot
    features = weight.shape[3]
    c_copies, w_copies = [], []
    for e, y in enumerate((side, 1 - side)):
        w_copies.append(
            start_copies(
                [
                    (weights[r].at[:, y], weight.at[e, :, aligned((quarter ^ r) * part, part)])
                    for r in range(4)
                ],
                w_sems,
                4 * e,
            )
        )
        pairs = []
        for k in range(units):
            source = unit ^ k
            at = aligned((source & 3) * slot, slot)
            for h in range(2):
                lanes = aligned((source >> 2) * 4 * own + h * 2 * own, 2 * own)
                pairs.append((contexts[(2 * h + e) * units + k], context.at[e, at, lanes]))
        c_copies.append(start_copies(pairs, c_sems, e * 2 * units))
    column = lax.broadcasted_iota(jnp.int32, (1, half), 1)
    row = lax.broadcasted_iota(jnp.int32, (half, half), 0)
    for turn in range(2):
        full, short = row_facts(lens, dest, group ^ turn, group, rows, slot)
        index = column - full[1]
        done = jnp.int32(0)
        for k in range(3):
            inside = jnp.logical_and(column >= short[k][1], column < short[k][1] + short[k][2])
            index = jnp.where(inside, slot + done + column - short[k][1], index)
            done = done + short[k][2]
        order[turn] = jnp.where(row == index, 1.0, 0.0).astype(BF16)
    sums = [None, None]
    sent = []
    for e in range(2):
        for copy in w_copies[e] + c_copies[e]:
            copy.wait()
        for turn in range(2):
            term = dot(
                context[e, turn * half : (turn + 1) * half],
                weight[e].reshape(units * own, features),
            )
            sums[turn] = term if e == 0 else sums[turn] + term
            if e:
                buf[turn] = dot(sums[turn].astype(BF16), order[turn], TN).astype(BF16)
                columns = aligned((group ^ turn) * half, half)
                sent += start_copies([(buf.at[turn], out.at[:, columns])], out_sems, turn)
    for copy in sent:
        copy.wait()


def output(place, lens, dest, weights, contexts, rows, slot):
    units, _, part, features = weights[0].shape
    tokens = BLOCKS * slot
    return pl.pallas_call(
        functools.partial(output_kernel, units, rows, slot),
        in_specs=[in_smem()] * 3 + [anywhere()] * (4 + len(contexts)),
        out_specs=anywhere(),
        out_shape=jax.ShapeDtypeStruct((features, tokens), BF16),
        scratch_shapes=[
            pltpu.VMEM((2, tokens, units * 4 * part), BF16),
            pltpu.VMEM((2, units, 4 * part, features), BF16),
            pltpu.VMEM((2, features, tokens // 2), BF16),
            pltpu.VMEM((2, tokens // 2, tokens // 2), BF16),
            pltpu.SemaphoreType.DMA((len(contexts),)),
            pltpu.SemaphoreType.DMA((8,)),
            pltpu.SemaphoreType.DMA((2,)),
        ],
        compiler_params=pltpu.CompilerParams(vmem_limit_bytes=VMEM),
        name="output",
    )(place, lens, dest, *weights, *contexts)


def swap(value, axis, mask=1):
    size = lax.axis_size(axis)
    return lax.ppermute(value, axis, [(i, i ^ mask) for i in range(size)])


def over_units(values):
    return [values[0]] + [swap(values[k], "tensor", 2 * k) for k in range(1, len(values))]


def all_quarters(value):
    across = swap(value, "parts")
    return [value, swap(value, "dp"), across, swap(across, "dp")]


def body(
    home,
    gain,
    q_values,
    q_scales,
    k_values,
    k_scales,
    v_values,
    v_scales,
    o_values,
    o_scales,
    row_lengths,
    row_dest,
):
    ranks = lax.axis_size("tensor")
    units = ranks // 2
    rank = lax.axis_index("tensor")
    unit, side = rank >> 1, rank & 1
    group = lax.axis_index("dp")
    quarter = (lax.axis_index("parts") & 1) * 2 + group
    features = home.shape[0]
    rows = row_lengths.shape[0] // 2
    slot = home.shape[1] // rows
    kv_head = rank * k_values.shape[0] // HD
    place = jnp.stack([jnp.asarray(v, jnp.int32) for v in (group, unit, side, quarter, kv_head)])

    keep, send, pos = deal(place, row_lengths, row_dest, home, rows, slot)
    pieces = weight_pieces(
        place, q_values, q_scales, k_values, k_scales, v_values, v_scales, units, [keep]
    )
    own_gain = lax.dynamic_slice_in_dim(
        gain.astype(F32), unit * 2 * features, 2 * features
    ).reshape(1, -1)
    frequency = rope_base ** (-2.0 * jnp.arange(HD // 2, dtype=F32) / HD)
    phases = pos[:, :1] * frequency[None, :]
    cosine, sine = jnp.cos(phases), jnp.sin(phases)
    part = HD // 4
    own_cos = lax.dynamic_slice_in_dim(cosine, side * part, part, 1)
    own_sin = lax.dynamic_slice_in_dim(sine, side * part, part, 1)
    own_cos = jnp.concatenate([own_cos] * 4, axis=1)
    own_sin = jnp.concatenate([-own_sin, own_sin] * 2, axis=1)
    wide_cos = jnp.concatenate([cosine, cosine], axis=1)
    wide_sin = jnp.concatenate([-sine, sine], axis=1)

    got = swap(send, "dp")
    o_pieces = output_pieces(place, o_values, o_scales, ranks, [got])
    keep2 = swap(keep, "tensor")
    got2 = lax.ppermute(
        send, ("dp", "tensor"), [(i, i ^ (ranks + 1)) for i in range(2 * ranks)]
    )
    own_piece, *pieces = over_units(pieces)
    own_pieces = [own_piece, swap(own_piece, "dp"), swap(own_piece, "parts")]
    collected, squares = collect(
        [keep, got, keep2, got2],
        pieces,
        [own_gain, own_cos, own_sin, wide_cos, wide_sin, o_pieces, *own_pieces[1:]],
    )

    squares = over_units([squares] * units)
    own_pieces.append(swap(own_pieces[2], "dp"))
    weights = [collected, swap(collected, "dp"), swap(collected, "parts")]
    (o_pieces,) = gate([o_pieces], squares[1:])
    o_moved = lax.all_to_all(o_pieces, "tensor", split_axis=0, concat_axis=0, tiled=True)
    normed = normalize(place, squares, own_gain, keep, got, keep2, got2)
    (weights[2],) = gate(weights[2:], [weights[1], own_pieces[3], normed])

    weights.append(swap(weights[2], "dp"))
    kept_a, near_a, kept_b, near_b = project(place, normed, own_pieces, weights, units)
    (o_moved,) = gate([o_moved], [kept_a])
    got_a = swap(near_a, "tensor", 2)
    (near_b,) = gate([near_b], [got_a])
    parts = []
    for kept, got in ((kept_a, got_a), (kept_b, swap(near_b, "tensor", 2))):
        sums = list(pair_sums(kept, got))
        far = [swap(value, "tensor", 4 * (i + 1)) for i, value in enumerate(sums)]
        parts.append([kept, got, *far])
    own_kv = key_value(parts[0], own_cos, own_sin, sums[:1])
    other_kv = swap(own_kv, "tensor")
    o_weights = [
        value.reshape(units, 2, *value.shape[1:]) for value in all_quarters(o_moved)
    ]
    contexts = []
    for h in range(2):
        query = queries(parts[h], wide_cos, wide_sin, near_b.shape[2], contexts[units : units + 1])
        context = attend(
            place, row_lengths, row_dest, query, own_kv, other_kv, h, rows, slot
        )
        mine, theirs = [context], [swap(context, "tensor")]
        for k in range(1, units):
            mine.append(swap(mine[k & (k - 1)], "tensor", 2 * (k & -k)))
            if k == 2:
                (mine[2],) = gate(mine[2:], [mine[1], theirs[0]])
        theirs += [swap(value, "tensor") for value in mine[1:]]
        contexts += mine + theirs
    return output(place, row_lengths, row_dest, o_weights, contexts, rows, slot)


def solution(mesh):
    in_specs = (
        P("tensor", ("parts", "dp")),
        P(),
        P(None, "tensor"),
        P(None, "tensor"),
        P("tensor", None),
        P(),
        P("tensor", None),
        P(),
        P("tensor", None),
        P("tensor", None),
        P("parts"),
        P("parts"),
    )
    out_specs = P("tensor", ("parts", "dp"))
    return jax.shard_map(body, mesh=mesh, in_specs=in_specs, out_specs=out_specs, check_vma=False)
```

```python
import functools
import math

import jax
import jax.numpy as jnp
from jax import lax
from jax.experimental import pallas as pl
from jax.experimental.pallas import tpu as pltpu
from jax.sharding import PartitionSpec as P

D = 8192
HD = 128
BLOCKS = 4

epsilon = 1e-06
rope_base = 1000000.0

F32 = jnp.float32
BF16 = jnp.bfloat16
NN = (((1,), (0,)), ((), ()))
NT = (((1,), (1,)), ((), ()))
TN = (((0,), (0,)), ((), ()))
VMEM = 40 << 20
ALL = 60 << 20


def dot(a, b, dims=NN):
    return lax.dot_general(a, b, dims, preferred_element_type=F32)


def in_vmem():
    return pl.BlockSpec(memory_space=pltpu.VMEM)


def in_smem():
    return pl.BlockSpec(memory_space=pltpu.SMEM)


def anywhere():
    return pl.BlockSpec(memory_space=pl.ANY)


def in_hbm():
    return pl.BlockSpec(memory_space=pltpu.HBM)


def start_copies(pairs, sems, first=0):
    copies = [
        pltpu.make_async_copy(source, target, sems.at[first + i])
        for i, (source, target) in enumerate(pairs)
    ]
    for copy in copies:
        copy.start()
    return copies


def aligned(value, size):
    return pl.ds(pl.multiple_of(value, size), size)


GROUP, UNIT, SIDE, QUARTER, KV_HEAD = range(5)


def row_facts(lens, dest, source, target, rows, slot):
    zero = jnp.int32(0)
    start, seen = zero, zero
    full = [zero, zero]
    short = [[zero, zero, zero] for _ in range(3)]
    for i in range(rows):
        mine = dest[source * rows + i] == target
        size = jnp.where(mine, lens[source * rows + i], 0)
        is_full = size == slot
        is_short = jnp.logical_and(mine, size != slot)
        full = [jnp.where(is_full, i, full[0]), jnp.where(is_full, start, full[1])]
        for k in range(3):
            hit = jnp.logical_and(is_short, seen == k)
            for e, value in enumerate((jnp.int32(i), start, size)):
                short[k][e] = jnp.where(hit, value, short[k][e])
        seen = seen + jnp.where(is_short, 1, 0)
        start = start + size
    return full, short


def pieces_kernel(units, count, place, qs, ks, vs, q_hbm, k_hbm, v_hbm, *rest):
    rest = rest[count:]
    outs = rest[:units]
    q_buf, k_buf, v_buf, pieces, in_sems, out_sems = rest[units:]
    unit, quarter, head = place[UNIT], place[QUARTER], place[KV_HEAD]
    _, size, own = q_buf.shape
    part = k_buf.shape[1]
    width = min(size, own)
    copies = []
    for k in range(units):
        at = ((unit ^ k) * 4 + quarter) * size
        copies.append(
            start_copies(
                [
                    (q_hbm.at[aligned(at, size)], q_buf.at[k]),
                    (k_hbm.at[:, aligned(at, size)], k_buf.at[k]),
                    (v_hbm.at[:, aligned(at, size)], v_buf.at[k]),
                ],
                in_sems,
                3 * k,
            )
        )
    sent = []
    for k in range(units):
        for copy in copies[k]:
            copy.wait()
        base = ((unit ^ k) * 4 + quarter) * (size // HD)
        for i in range(size // HD):
            rows = slice(i * HD, (i + 1) * HD)
            for h in range(own // HD):
                cols = slice(h * HD, (h + 1) * HD)
                scaled = q_buf[k, rows, cols].astype(F32) * qs[h, base + i]
                pieces[k, rows, cols] = scaled.astype(BF16)
            turn, lane = divmod(i * HD, width)
            at = size + 2 * part * turn
            lanes = slice(lane, lane + HD)
            pieces[k, at : at + part, lanes] = (
                k_buf[k, :, rows].astype(F32) * ks[head, base + i]
            ).astype(BF16)
            pieces[k, at + part : at + 2 * part, lanes] = (
                v_buf[k, :, rows].astype(F32) * vs[head, base + i]
            ).astype(BF16)
        if width < own:
            pieces[k, size:, width:] = jnp.zeros((2 * part, own - width), BF16)
        sent += start_copies([(pieces.at[k], outs[k])], out_sems, k)
    for copy in sent:
        copy.wait()


def weight_pieces(place, q_values, q_scales, k_values, k_scales, v_values, v_scales, units, after):
    own = q_values.shape[1]
    part = k_values.shape[0]
    size = q_values.shape[0] // units // 4
    rows = size + 2 * part * max(1, size // own)
    return pl.pallas_call(
        functools.partial(pieces_kernel, units, len(after)),
        in_specs=[in_smem()] * 4 + [in_hbm()] * 3 + [anywhere()] * len(after),
        out_specs=[anywhere()] * units,
        out_shape=[jax.ShapeDtypeStruct((rows, own), BF16)] * units,
        scratch_shapes=[
            pltpu.VMEM((units, size, own), BF16),
            pltpu.VMEM((units, part, size), BF16),
            pltpu.VMEM((units, part, size), BF16),
            pltpu.VMEM((units, rows, own), BF16),
            pltpu.SemaphoreType.DMA((3 * units,)),
            pltpu.SemaphoreType.DMA((units,)),
        ],
        compiler_params=pltpu.CompilerParams(vmem_limit_bytes=ALL),
        name="weight_pieces",
    )(place, q_scales.T, k_scales, v_scales, q_values, k_values, v_values, *after)


def o_pieces_kernel(count, place, scales, o_hbm, *rest):
    out, token, o_buf, pieces, sem, out_sem = rest[count:]
    token[...] = jnp.zeros_like(token)
    ranks, rows, features = pieces.shape
    first = place[QUARTER] * rows
    (copy,) = start_copies([(o_hbm.at[aligned(first, rows)], o_buf)], sem)
    copy.wait()
    for rank in range(ranks):
        for i in range(features // HD):
            block = rank * (features // HD) + i
            scaled = o_buf[:, block * HD : (block + 1) * HD].astype(F32) * scales[first // HD, block]
            pieces[rank, :, i * HD : (i + 1) * HD] = scaled.astype(BF16)
    (sent,) = start_copies([(pieces, out)], out_sem)
    sent.wait()


def output_pieces(place, o_values, o_scales, ranks, after):
    shape = (ranks, o_values.shape[0] // 4, o_values.shape[1] // ranks)
    return pl.pallas_call(
        functools.partial(o_pieces_kernel, len(after)),
        in_specs=[in_smem()] * 2 + [in_hbm()] + [anywhere()] * len(after),
        out_specs=[anywhere(), in_vmem()],
        out_shape=[jax.ShapeDtypeStruct(shape, BF16), jax.ShapeDtypeStruct((8, 128), F32)],
        scratch_shapes=[
            pltpu.VMEM((shape[1], o_values.shape[1]), BF16),
            pltpu.VMEM(shape, BF16),
            pltpu.SemaphoreType.DMA((1,)),
            pltpu.SemaphoreType.DMA((1,)),
        ],
        compiler_params=pltpu.CompilerParams(vmem_limit_bytes=ALL),
        name="output_pieces",
    )(place, o_scales, o_values, *after)


def deal_kernel(rows, slot, place, lens, dest, home, keep, send, pos, pick):
    step = pl.program_id(0)
    group, block = place[GROUP], place[UNIT] & (BLOCKS - 1)

    @pl.when(step == 0)
    def _():
        column = lax.broadcasted_iota(jnp.int32, (slot, 1), 0)
        lane = lax.broadcasted_iota(jnp.int32, (slot, rows * slot), 1)
        for turn in range(2):
            full, short = row_facts(lens, dest, group, group ^ turn, rows, slot)
            first = short[0][2]
            second = first + short[1][2]
            from_short = jnp.where(
                column < first,
                short[0][0] * slot + column,
                jnp.where(
                    column < second,
                    short[1][0] * slot + column - first,
                    short[2][0] * slot + column - second,
                ),
            )
            for kind, index in enumerate((full[0] * slot + column, from_short)):
                at = (turn * 2 + kind) * slot
                pick[at : at + slot, :] = jnp.where(lane == index, 1.0, 0.0).astype(BF16)
        _, short = row_facts(lens, dest, group ^ (block >> 1), group, rows, slot)
        first = short[0][2]
        second = first + short[1][2]
        begin = jnp.where(column < first, 0, jnp.where(column < second, first, second))
        place_in_row = column - jnp.where((block & 1) == 1, begin, 0)
        pos[...] = jnp.broadcast_to(place_in_row.astype(F32), pos.shape)

    taken = dot(pick[...], home[...], NT)
    half = 2 * slot
    keep[...] = taken[:half].astype(BF16)
    send[...] = taken[half:].astype(BF16)


def deal(place, lens, dest, home, rows, slot):
    features = home.shape[0]
    width = min(features, 256)
    tokens = BLOCKS * slot
    return pl.pallas_call(
        functools.partial(deal_kernel, rows, slot),
        grid=(features // width,),
        in_specs=[
            in_smem(),
            in_smem(),
            in_smem(),
            pl.BlockSpec((width, home.shape[1]), lambda i: (i, 0)),
        ],
        out_specs=[
            pl.BlockSpec((tokens // 2, width), lambda i: (0, i)),
            pl.BlockSpec((tokens // 2, width), lambda i: (0, i)),
            pl.BlockSpec((slot, 128), lambda i: (0, 0)),
        ],
        out_shape=[
            jax.ShapeDtypeStruct((tokens // 2, features), BF16),
            jax.ShapeDtypeStruct((tokens // 2, features), BF16),
            jax.ShapeDtypeStruct((slot, 128), F32),
        ],
        scratch_shapes=[
            pltpu.VMEM((tokens, rows * slot), BF16),
        ],
        compiler_params=pltpu.CompilerParams(vmem_limit_bytes=ALL),
        name="deal",
    )(place, lens, dest, home)


def collect_kernel(count, extra, *refs):
    tokens, pieces = refs[:4], refs[4 : 4 + count]
    out, sums = refs[4 + count + extra : 6 + count + extra]
    x_buf, buf, x_sems, sems, out_sems = refs[-5:]
    copies = start_copies([(ref, buf.at[k]) for k, ref in enumerate(pieces)], sems)
    x_copies = start_copies([(ref, x_buf.at[i]) for i, ref in enumerate(tokens)], x_sems)
    sent = []
    for k, copy in enumerate(copies):
        copy.wait()
        sent += start_copies([(buf.at[k], out.at[k])], out_sems, k)
    _, half, features = x_buf.shape
    for i in range(2):
        total = None
        for j in (i, i + 2):
            x_copies[j].wait()
            for at in range(features // 128):
                piece = x_buf[j, :, at * 128 : (at + 1) * 128].astype(F32)
                total = piece * piece if total is None else total + piece * piece
        sums[:, i * half : (i + 1) * half] = jnp.broadcast_to(
            jnp.sum(total.T, axis=0, keepdims=True), (8, half)
        )
    for copy in sent:
        copy.wait()


def collect(tokens, pieces, after):
    count = len(pieces)
    half, features = tokens[0].shape
    return pl.pallas_call(
        functools.partial(collect_kernel, count, len(after)),
        in_specs=[anywhere()] * (4 + count + len(after)),
        out_specs=[anywhere(), in_vmem()],
        out_shape=[
            jax.ShapeDtypeStruct((count, *pieces[0].shape), BF16),
            jax.ShapeDtypeStruct((8, 2 * half), F32),
        ],
        scratch_shapes=[
            pltpu.VMEM((4, half, features), BF16),
            pltpu.VMEM((count, *pieces[0].shape), BF16),
            pltpu.SemaphoreType.DMA((4,)),
            pltpu.SemaphoreType.DMA((count,)),
            pltpu.SemaphoreType.DMA((count,)),
        ],
        compiler_params=pltpu.CompilerParams(vmem_limit_bytes=ALL),
        name="collect",
    )(*tokens, *pieces, *after)


def gate_kernel(*refs):
    pass


def gate(through, after):
    count = len(through)
    return pl.pallas_call(
        gate_kernel,
        in_specs=[anywhere()] * (count + len(after)),
        out_specs=[anywhere()] * count,
        out_shape=[jax.ShapeDtypeStruct(value.shape, value.dtype) for value in through],
        input_output_aliases={i: i for i in range(count)},
        compiler_params=pltpu.CompilerParams(vmem_limit_bytes=VMEM),
        name="gate",
    )(*through, *after)


def normalize_kernel(units, place, *rest):
    squares, (gain, keep, got, keep2, got2) = rest[:units], rest[units : units + 5]
    out, x_buf, normed, x_sems, out_sems = rest[units + 5 :]
    side = place[SIDE]
    _, half, features = x_buf.shape
    copies = start_copies(
        [(ref, x_buf.at[i]) for i, ref in enumerate((keep, got, keep2, got2))], x_sems
    )
    total = squares[0][...]
    for ref in squares[1:]:
        total = total + ref[...]
    inverse = lax.rsqrt(total / D + epsilon).T[:, :1]
    sent = []
    for i in range(4):
        at = side if i < 2 else 1 - side
        lanes = aligned(at * features, features)
        rows = slice((i & 1) * half, ((i & 1) + 1) * half)
        copies[i].wait()
        wide_rows = x_buf[i].astype(F32)
        normed[i] = (wide_rows * inverse[rows] * gain[:, lanes]).astype(BF16)
        sent += start_copies([(normed.at[i], out.at[rows, lanes])], out_sems, i)
    for copy in sent:
        copy.wait()


def normalize(place, squares, gain, keep, got, keep2, got2):
    half, features = keep.shape
    return pl.pallas_call(
        functools.partial(normalize_kernel, len(squares)),
        in_specs=[in_smem()] + [in_vmem()] * (len(squares) + 1) + [anywhere()] * 4,
        out_specs=anywhere(),
        out_shape=jax.ShapeDtypeStruct((2 * half, 2 * features), BF16),
        scratch_shapes=[
            pltpu.VMEM((4, half, features), BF16),
            pltpu.VMEM((4, half, features), BF16),
            pltpu.SemaphoreType.DMA((4,)),
            pltpu.SemaphoreType.DMA((4,)),
        ],
        compiler_params=pltpu.CompilerParams(vmem_limit_bytes=VMEM),
        name="normalize",
    )(place, *squares, gain, keep, got, keep2, got2)


def project_kernel(units, place, tokens, *rest):
    own_pieces, weights, outs = rest[:4], rest[4:8], rest[8:12]
    buf, out_sems = rest[12:]
    unit, quarter = place[UNIT], place[QUARTER]
    count, wide = tokens.shape
    slot = count // BLOCKS
    rows, own = own_pieces[0].shape
    size = wide // 4
    width = min(size, own)
    part = (rows - size) // (size // width)

    def weight(k, r, rows, lanes=slice(None)):
        return weights[r][k - 1, rows, lanes] if k else own_pieces[r][rows, lanes]

    def features(r, first, count):
        return tokens[:, aligned((quarter ^ r) * size + first, count)]

    sent = []

    def hand_out(group, cols, index, chunk, place_in_chunk):
        for k in range(4 * group, 4 * group + 4):
            rows = aligned(((unit ^ k) & 3) * slot, slot)
            target = outs[2 * chunk + (k & 1)].at[k >> 1, :, place_in_chunk]
            sent.extend(start_copies([(buf.at[group, rows, cols], target)], out_sems, 3 * k + index))

    for group in range(units // BLOCKS):
        members = range(4 * group, 4 * group + 4)
        for k in members:
            s = (unit ^ k) & 3
            value = None
            for r in range(4):
                term = dot(features(r, 0, size), weight(k, r, slice(0, size)))
                value = term if value is None else value + term
            buf[group, :, aligned(s * own, own)] = value.astype(BF16)
        hand_out(group, slice(0, 2 * own), 0, 0, slice(0, 2 * own))
        hand_out(group, slice(2 * own, 4 * own), 1, 1, slice(0, 2 * own))
        value = None
        for r in range(4):
            for e in range(size // width):
                pieces = []
                for half in range(2):
                    first = size + e * part + half * (part // 2)
                    rows, lanes = slice(first, first + part // 2), slice(0, width)
                    for s in range(4):
                        k = 4 * group + ((unit & 3) ^ s)
                        piece = weights[r][jnp.maximum(k - 1, 0), rows, lanes]
                        if group == 0:
                            piece = jnp.where(k == 0, own_pieces[r][rows, lanes], piece)
                        pieces.append(piece)
                w = jnp.concatenate(pieces, axis=0)
                term = dot(features(r, e * width, width), w, NT)
                value = term if value is None else value + term
        buf[group, :, 4 * own :] = value.astype(BF16)
        cols = slice(4 * own, 4 * own + 4 * part)
        hand_out(group, cols, 2, 0, slice(2 * own, 2 * own + 4 * part))
    for copy in sent:
        copy.wait()


def project(place, normed, own_pieces, weights, units):
    tokens, wide = normed.shape
    slot = tokens // BLOCKS
    rows, own = own_pieces[0].shape
    size = wide // 4
    part = (rows - size) // (size // min(size, own))
    groups = units // BLOCKS
    outs = pl.pallas_call(
        functools.partial(project_kernel, units),
        in_specs=[in_smem()] + [in_vmem()] * 9,
        out_specs=[anywhere()] * 4,
        out_shape=[jax.ShapeDtypeStruct((units // 2, slot, 2 * own + 4 * part), BF16)] * 2
        + [jax.ShapeDtypeStruct((units // 2, slot, 2 * own), BF16)] * 2,
        scratch_shapes=[
            pltpu.VMEM((groups, tokens, 4 * own + 4 * part), BF16),
            pltpu.SemaphoreType.DMA((3 * units,)),
        ],
        compiler_params=pltpu.CompilerParams(vmem_limit_bytes=VMEM),
        name="project",
    )(place, normed, *own_pieces, *weights)
    return outs


def pair_sum_kernel(kept, got, *outs):
    for i, out in enumerate(outs):
        out[...] = (kept[i + 1].astype(F32) + got[i + 1].astype(F32)).astype(BF16)


def pair_sums(kept, got):
    count = kept.shape[0] - 1
    return pl.pallas_call(
        pair_sum_kernel,
        in_specs=[in_vmem()] * 2,
        out_specs=[in_vmem()] * count,
        out_shape=[jax.ShapeDtypeStruct(kept.shape[1:], BF16)] * count,
        compiler_params=pltpu.CompilerParams(vmem_limit_bytes=VMEM),
        name="pair_sums",
    )(kept, got)


def all_parts(refs, cols):
    kept, got = refs[:2]
    value = kept[0, :, cols].astype(F32) + got[0, :, cols].astype(F32)
    for ref in refs[2:]:
        value = value + ref[:, cols].astype(F32)
    return value.astype(BF16).astype(F32)


def key_value_kernel(count, cosine, sine, *refs):
    parts, out = refs[:count], refs[-1]
    wide = parts[0].shape[2]
    value = all_parts(parts, slice(wide - out.shape[1], wide))
    keys, values = value[:, :HD], value[:, HD:]
    part = HD // 4
    lane = lax.broadcasted_iota(jnp.int32, keys.shape, 1)
    odd = (lane & part) != 0
    swapped = jnp.where(odd, pltpu.roll(keys, part, 1), pltpu.roll(keys, HD - part, 1))
    out[:, :HD] = (keys * cosine[...] + swapped * sine[...]).astype(BF16)
    out[:, HD:] = values.astype(BF16)


def key_value(parts, cosine, sine, after):
    return pl.pallas_call(
        functools.partial(key_value_kernel, len(parts)),
        in_specs=[in_vmem()] * (2 + len(parts)) + [anywhere()] * len(after),
        out_specs=in_vmem(),
        out_shape=jax.ShapeDtypeStruct((parts[0].shape[1], parts[0].shape[2] // 3), BF16),
        compiler_params=pltpu.CompilerParams(vmem_limit_bytes=VMEM),
        name="key_value",
    )(cosine, sine, *parts, *after)


def query_kernel(count, cosine, sine, *refs):
    parts, out = refs[:count], refs[-1]
    cos, sin = cosine[...], sine[...]
    for head in range(out.shape[1] // HD):
        at = slice(head * HD, (head + 1) * HD)
        query = all_parts(parts, at)
        out[:, at] = (query * cos + pltpu.roll(query, HD // 2, 1) * sin).astype(BF16)


def queries(parts, cosine, sine, wide, after):
    return pl.pallas_call(
        functools.partial(query_kernel, len(parts)),
        in_specs=[in_vmem()] * (2 + len(parts)) + [anywhere()] * len(after),
        out_specs=in_vmem(),
        out_shape=jax.ShapeDtypeStruct((parts[0].shape[1], wide), BF16),
        compiler_params=pltpu.CompilerParams(vmem_limit_bytes=VMEM),
        name="queries",
    )(cosine, sine, *parts, *after)


def attend_kernel(kv_head, rows, slot, place, lens, dest, query, own_kv, other_kv, out):
    group, block, side = place[GROUP], place[UNIT] & (BLOCKS - 1), place[SIDE]
    _, short = row_facts(lens, dest, group ^ (block >> 1), group, rows, slot)
    many = (block & 1) == 1
    first = jnp.where(many, short[0][2], slot)
    second = jnp.where(many, first + short[1][2], slot)

    def segment(shape, axis):
        at = lax.broadcasted_iota(jnp.int32, shape, axis)
        return jnp.where(at >= first, 1, 0) + jnp.where(at >= second, 1, 0)

    shape = (slot, slot)
    allowed = jnp.logical_and(
        segment(shape, 0) == segment(shape, 1),
        lax.broadcasted_iota(jnp.int32, shape, 1) <= lax.broadcasted_iota(jnp.int32, shape, 0),
    )
    mine, theirs = own_kv[...].astype(F32), other_kv[...].astype(F32)
    even = jnp.where(side == 0, mine, theirs)
    odd = jnp.where(side == 0, theirs, mine)
    part = HD // 4

    def whole_head(index):
        pieces = []
        for b in range(2):
            at = slice((2 * index + b) * part, (2 * index + b + 1) * part)
            pieces += [even[:, at], odd[:, at]]
        return jnp.concatenate(pieces, axis=1).astype(BF16)

    key, value = whole_head(kv_head), whole_head(2 + kv_head)
    scale = 1.0 / math.sqrt(HD)
    for head in range(out.shape[1] // HD):
        at = slice(head * HD, (head + 1) * HD)
        scores = dot(query[:, at], key, NT) * scale
        scores = jnp.where(allowed, scores, -1e30)
        weights = jnp.exp(scores - jnp.max(scores, axis=1, keepdims=True))
        attention = (weights / jnp.sum(weights, axis=1, keepdims=True)).astype(BF16)
        out[:, at] = dot(attention, value).astype(BF16)


def attend(place, lens, dest, query, own_kv, other_kv, kv_head, rows, slot):
    return pl.pallas_call(
        functools.partial(attend_kernel, kv_head, rows, slot),
        in_specs=[in_smem()] * 3 + [in_vmem()] * 3,
        out_specs=in_vmem(),
        out_shape=jax.ShapeDtypeStruct(query.shape, BF16),
        compiler_params=pltpu.CompilerParams(vmem_limit_bytes=VMEM),
        name="attend",
    )(place, lens, dest, query, own_kv, other_kv)


def output_kernel(units, rows, slot, place, lens, dest, *refs):
    weights, contexts = refs[:4], refs[4 : 4 + 4 * units]
    out, context, weight, buf, order, c_sems, w_sems, out_sems = refs[4 + 4 * units :]
    unit, side, quarter, group = place[UNIT], place[SIDE], place[QUARTER], place[GROUP]
    part = weights[0].shape[2]
    own = 4 * part
    half = 2 * slot
    features = weight.shape[3]
    c_copies, w_copies = [], []
    for e, y in enumerate((side, 1 - side)):
        w_copies.append(
            start_copies(
                [
                    (weights[r].at[:, y], weight.at[e, :, aligned((quarter ^ r) * part, part)])
                    for r in range(4)
                ],
                w_sems,
                4 * e,
            )
        )
        pairs = []
        for k in range(units):
            source = unit ^ k
            at = aligned((source & 3) * slot, slot)
            for h in range(2):
                lanes = aligned((source >> 2) * 4 * own + h * 2 * own, 2 * own)
                pairs.append((contexts[(2 * h + e) * units + k], context.at[e, at, lanes]))
        c_copies.append(start_copies(pairs, c_sems, e * 2 * units))
    column = lax.broadcasted_iota(jnp.int32, (1, half), 1)
    row = lax.broadcasted_iota(jnp.int32, (half, half), 0)
    for turn in range(2):
        full, short = row_facts(lens, dest, group ^ turn, group, rows, slot)
        index = column - full[1]
        done = jnp.int32(0)
        for k in range(3):
            inside = jnp.logical_and(column >= short[k][1], column < short[k][1] + short[k][2])
            index = jnp.where(inside, slot + done + column - short[k][1], index)
            done = done + short[k][2]
        order[turn] = jnp.where(row == index, 1.0, 0.0).astype(BF16)
    sums = [None, None]
    sent = []
    for e in range(2):
        for copy in w_copies[e] + c_copies[e]:
            copy.wait()
        for turn in range(2):
            term = dot(
                context[e, turn * half : (turn + 1) * half],
                weight[e].reshape(units * own, features),
            )
            sums[turn] = term if e == 0 else sums[turn] + term
            if e:
                buf[turn] = dot(sums[turn].astype(BF16), order[turn], TN).astype(BF16)
                columns = aligned((group ^ turn) * half, half)
                sent += start_copies([(buf.at[turn], out.at[:, columns])], out_sems, turn)
    for copy in sent:
        copy.wait()


def output(place, lens, dest, weights, contexts, rows, slot):
    units, _, part, features = weights[0].shape
    tokens = BLOCKS * slot
    return pl.pallas_call(
        functools.partial(output_kernel, units, rows, slot),
        in_specs=[in_smem()] * 3 + [anywhere()] * (4 + len(contexts)),
        out_specs=anywhere(),
        out_shape=jax.ShapeDtypeStruct((features, tokens), BF16),
        scratch_shapes=[
            pltpu.VMEM((2, tokens, units * 4 * part), BF16),
            pltpu.VMEM((2, units, 4 * part, features), BF16),
            pltpu.VMEM((2, features, tokens // 2), BF16),
            pltpu.VMEM((2, tokens // 2, tokens // 2), BF16),
            pltpu.SemaphoreType.DMA((len(contexts),)),
            pltpu.SemaphoreType.DMA((8,)),
            pltpu.SemaphoreType.DMA((2,)),
        ],
        compiler_params=pltpu.CompilerParams(vmem_limit_bytes=VMEM),
        name="output",
    )(place, lens, dest, *weights, *contexts)


def swap(value, axis, mask=1):
    size = lax.axis_size(axis)
    return lax.ppermute(value, axis, [(i, i ^ mask) for i in range(size)])


def over_units(values):
    return [values[0]] + [swap(values[k], "tensor", 2 * k) for k in range(1, len(values))]


def all_quarters(value):
    across = swap(value, "parts")
    return [value, swap(value, "dp"), across, swap(across, "dp")]


def body(
    home,
    gain,
    q_values,
    q_scales,
    k_values,
    k_scales,
    v_values,
    v_scales,
    o_values,
    o_scales,
    row_lengths,
    row_dest,
):
    ranks = lax.axis_size("tensor")
    units = ranks // 2
    rank = lax.axis_index("tensor")
    unit, side = rank >> 1, rank & 1
    group = lax.axis_index("dp")
    quarter = (lax.axis_index("parts") & 1) * 2 + group
    features = home.shape[0]
    rows = row_lengths.shape[0] // 2
    slot = home.shape[1] // rows
    kv_head = rank * k_values.shape[0] // HD
    place = jnp.stack([jnp.asarray(v, jnp.int32) for v in (group, unit, side, quarter, kv_head)])

    keep, send, pos = deal(place, row_lengths, row_dest, home, rows, slot)
    pieces = weight_pieces(
        place, q_values, q_scales, k_values, k_scales, v_values, v_scales, units, [keep]
    )
    own_gain = lax.dynamic_slice_in_dim(
        gain.astype(F32), unit * 2 * features, 2 * features
    ).reshape(1, -1)
    frequency = rope_base ** (-2.0 * jnp.arange(HD // 2, dtype=F32) / HD)
    phases = pos[:, :1] * frequency[None, :]
    cosine, sine = jnp.cos(phases), jnp.sin(phases)
    part = HD // 4
    own_cos = lax.dynamic_slice_in_dim(cosine, side * part, part, 1)
    own_sin = lax.dynamic_slice_in_dim(sine, side * part, part, 1)
    own_cos = jnp.concatenate([own_cos] * 4, axis=1)
    own_sin = jnp.concatenate([-own_sin, own_sin] * 2, axis=1)
    wide_cos = jnp.concatenate([cosine, cosine], axis=1)
    wide_sin = jnp.concatenate([-sine, sine], axis=1)

    got = swap(send, "dp")
    o_pieces, o_made = output_pieces(place, o_values, o_scales, ranks, [got])
    keep2 = swap(keep, "tensor")
    got2 = lax.ppermute(
        send, ("dp", "tensor"), [(i, i ^ (ranks + 1)) for i in range(2 * ranks)]
    )
    own_piece, *pieces = over_units(pieces)
    own_pieces = [own_piece, swap(own_piece, "dp"), swap(own_piece, "parts")]
    collected, squares = collect(
        [keep, got, keep2, got2],
        pieces,
        [own_gain, own_cos, own_sin, wide_cos, wide_sin, o_made, *own_pieces[1:]],
    )

    squares = over_units([squares] * units)
    own_pieces.append(swap(own_pieces[2], "dp"))
    weights = [collected, swap(collected, "dp"), swap(collected, "parts")]
    (o_pieces,) = gate([o_pieces], squares[1:])
    o_moved = lax.all_to_all(o_pieces, "tensor", split_axis=0, concat_axis=0, tiled=True)
    normed = normalize(place, squares, own_gain, keep, got, keep2, got2)
    (weights[2],) = gate(weights[2:], [weights[1], own_pieces[3], normed])

    weights.append(swap(weights[2], "dp"))
    kept_a, near_a, kept_b, near_b = project(place, normed, own_pieces, weights, units)
    (o_moved,) = gate([o_moved], [kept_a])
    got_a = swap(near_a, "tensor", 2)
    (near_b,) = gate([near_b], [got_a])
    parts = []
    for kept, got in ((kept_a, got_a), (kept_b, swap(near_b, "tensor", 2))):
        sums = list(pair_sums(kept, got))
        far = [swap(value, "tensor", 4 * (i + 1)) for i, value in enumerate(sums)]
        parts.append([kept, got, *far])
    own_kv = key_value(parts[0], own_cos, own_sin, sums[:1])
    other_kv = swap(own_kv, "tensor")
    o_weights = [
        value.reshape(units, 2, *value.shape[1:]) for value in all_quarters(o_moved)
    ]
    contexts = []
    for h in range(2):
        query = queries(parts[h], wide_cos, wide_sin, near_b.shape[2], contexts[units : units + 1])
        context = attend(
            place, row_lengths, row_dest, query, own_kv, other_kv, h, rows, slot
        )
        mine, theirs = [context], [swap(context, "tensor")]
        for k in range(1, units):
            mine.append(swap(mine[k & (k - 1)], "tensor", 2 * (k & -k)))
            if k == 2:
                (mine[2],) = gate(mine[2:], [mine[1], theirs[0]])
        theirs += [swap(value, "tensor") for value in mine[1:]]
        contexts += mine + theirs
    return output(place, row_lengths, row_dest, o_weights, contexts, rows, slot)


def solution(mesh):
    in_specs = (
        P("tensor", ("parts", "dp")),
        P(),
        P(None, "tensor"),
        P(None, "tensor"),
        P("tensor", None),
        P(),
        P("tensor", None),
        P(),
        P("tensor", None),
        P("tensor", None),
        P("parts"),
        P("parts"),
    )
    out_specs = P("tensor", ("parts", "dp"))
    return jax.shard_map(body, mesh=mesh, in_specs=in_specs, out_specs=out_specs, check_vma=False)
```

```python
import functools
import math

import jax
import jax.numpy as jnp
from jax import lax
from jax.experimental import pallas as pl
from jax.experimental.pallas import tpu as pltpu
from jax.sharding import PartitionSpec as P

D = 8192
HD = 128
BLOCKS = 4

epsilon = 1e-06
rope_base = 1000000.0

F32 = jnp.float32
BF16 = jnp.bfloat16
NN = (((1,), (0,)), ((), ()))
NT = (((1,), (1,)), ((), ()))
TN = (((0,), (0,)), ((), ()))
VMEM = 40 << 20
ALL = 60 << 20


def dot(a, b, dims=NN):
    return lax.dot_general(a, b, dims, preferred_element_type=F32)


def in_vmem():
    return pl.BlockSpec(memory_space=pltpu.VMEM)


def in_smem():
    return pl.BlockSpec(memory_space=pltpu.SMEM)


def anywhere():
    return pl.BlockSpec(memory_space=pl.ANY)


def in_hbm():
    return pl.BlockSpec(memory_space=pltpu.HBM)


def start_copies(pairs, sems, first=0):
    copies = [
        pltpu.make_async_copy(source, target, sems.at[first + i])
        for i, (source, target) in enumerate(pairs)
    ]
    for copy in copies:
        copy.start()
    return copies


def aligned(value, size):
    return pl.ds(pl.multiple_of(value, size), size)


GROUP, UNIT, SIDE, QUARTER, KV_HEAD = range(5)


def row_facts(lens, dest, source, target, rows, slot):
    zero = jnp.int32(0)
    start, seen = zero, zero
    full = [zero, zero]
    short = [[zero, zero, zero] for _ in range(3)]
    for i in range(rows):
        mine = dest[source * rows + i] == target
        size = jnp.where(mine, lens[source * rows + i], 0)
        is_full = size == slot
        is_short = jnp.logical_and(mine, size != slot)
        full = [jnp.where(is_full, i, full[0]), jnp.where(is_full, start, full[1])]
        for k in range(3):
            hit = jnp.logical_and(is_short, seen == k)
            for e, value in enumerate((jnp.int32(i), start, size)):
                short[k][e] = jnp.where(hit, value, short[k][e])
        seen = seen + jnp.where(is_short, 1, 0)
        start = start + size
    return full, short


def pieces_kernel(units, count, place, qs, ks, vs, q_hbm, k_hbm, v_hbm, *rest):
    rest = rest[count:]
    outs = rest[:units]
    q_buf, k_buf, v_buf, pieces, in_sems, out_sems = rest[units:]
    unit, quarter, head = place[UNIT], place[QUARTER], place[KV_HEAD]
    _, size, own = q_buf.shape
    part = k_buf.shape[1]
    width = min(size, own)
    copies = []
    for k in range(units):
        at = ((unit ^ k) * 4 + quarter) * size
        copies.append(
            start_copies(
                [
                    (q_hbm.at[aligned(at, size)], q_buf.at[k]),
                    (k_hbm.at[:, aligned(at, size)], k_buf.at[k]),
                    (v_hbm.at[:, aligned(at, size)], v_buf.at[k]),
                ],
                in_sems,
                3 * k,
            )
        )
    sent = []
    for k in range(units):
        for copy in copies[k]:
            copy.wait()
        base = ((unit ^ k) * 4 + quarter) * (size // HD)
        for i in range(size // HD):
            rows = slice(i * HD, (i + 1) * HD)
            for h in range(own // HD):
                cols = slice(h * HD, (h + 1) * HD)
                scaled = q_buf[k, rows, cols].astype(F32) * qs[h, base + i]
                pieces[k, rows, cols] = scaled.astype(BF16)
            turn, lane = divmod(i * HD, width)
            at = size + 2 * part * turn
            lanes = slice(lane, lane + HD)
            pieces[k, at : at + part, lanes] = (
                k_buf[k, :, rows].astype(F32) * ks[head, base + i]
            ).astype(BF16)
            pieces[k, at + part : at + 2 * part, lanes] = (
                v_buf[k, :, rows].astype(F32) * vs[head, base + i]
            ).astype(BF16)
        if width < own:
            pieces[k, size:, width:] = jnp.zeros((2 * part, own - width), BF16)
        sent += start_copies([(pieces.at[k], outs[k])], out_sems, k)
    for copy in sent:
        copy.wait()


def weight_pieces(place, q_values, q_scales, k_values, k_scales, v_values, v_scales, units, after):
    own = q_values.shape[1]
    part = k_values.shape[0]
    size = q_values.shape[0] // units // 4
    rows = size + 2 * part * max(1, size // own)
    return pl.pallas_call(
        functools.partial(pieces_kernel, units, len(after)),
        in_specs=[in_smem()] * 4 + [in_hbm()] * 3 + [anywhere()] * len(after),
        out_specs=[anywhere()] * units,
        out_shape=[jax.ShapeDtypeStruct((rows, own), BF16)] * units,
        scratch_shapes=[
            pltpu.VMEM((units, size, own), BF16),
            pltpu.VMEM((units, part, size), BF16),
            pltpu.VMEM((units, part, size), BF16),
            pltpu.VMEM((units, rows, own), BF16),
            pltpu.SemaphoreType.DMA((3 * units,)),
            pltpu.SemaphoreType.DMA((units,)),
        ],
        compiler_params=pltpu.CompilerParams(vmem_limit_bytes=ALL),
        name="weight_pieces",
    )(place, q_scales.T, k_scales, v_scales, q_values, k_values, v_values, *after)


def o_pieces_kernel(count, place, scales, o_hbm, *rest):
    out, token, o_buf, pieces, sem, out_sem = rest[count:]
    token[...] = jnp.zeros_like(token)
    ranks, rows, features = pieces.shape
    first = place[QUARTER] * rows
    (copy,) = start_copies([(o_hbm.at[aligned(first, rows)], o_buf)], sem)
    copy.wait()
    for rank in range(ranks):
        for i in range(features // HD):
            block = rank * (features // HD) + i
            scaled = o_buf[:, block * HD : (block + 1) * HD].astype(F32) * scales[first // HD, block]
            pieces[rank, :, i * HD : (i + 1) * HD] = scaled.astype(BF16)
    (sent,) = start_copies([(pieces, out)], out_sem)
    sent.wait()


def output_pieces(place, o_values, o_scales, ranks, after):
    shape = (ranks, o_values.shape[0] // 4, o_values.shape[1] // ranks)
    return pl.pallas_call(
        functools.partial(o_pieces_kernel, len(after)),
        in_specs=[in_smem()] * 2 + [in_hbm()] + [anywhere()] * len(after),
        out_specs=[anywhere(), in_vmem()],
        out_shape=[jax.ShapeDtypeStruct(shape, BF16), jax.ShapeDtypeStruct((8, 128), F32)],
        scratch_shapes=[
            pltpu.VMEM((shape[1], o_values.shape[1]), BF16),
            pltpu.VMEM(shape, BF16),
            pltpu.SemaphoreType.DMA((1,)),
            pltpu.SemaphoreType.DMA((1,)),
        ],
        compiler_params=pltpu.CompilerParams(vmem_limit_bytes=ALL),
        name="output_pieces",
    )(place, o_scales, o_values, *after)


def deal_kernel(rows, slot, place, lens, dest, home, keep, send, pos, pick):
    step = pl.program_id(0)
    group, block = place[GROUP], place[UNIT] & (BLOCKS - 1)

    @pl.when(step == 0)
    def _():
        column = lax.broadcasted_iota(jnp.int32, (slot, 1), 0)
        lane = lax.broadcasted_iota(jnp.int32, (slot, rows * slot), 1)
        for turn in range(2):
            full, short = row_facts(lens, dest, group, group ^ turn, rows, slot)
            first = short[0][2]
            second = first + short[1][2]
            from_short = jnp.where(
                column < first,
                short[0][0] * slot + column,
                jnp.where(
                    column < second,
                    short[1][0] * slot + column - first,
                    short[2][0] * slot + column - second,
                ),
            )
            for kind, index in enumerate((full[0] * slot + column, from_short)):
                at = (turn * 2 + kind) * slot
                pick[at : at + slot, :] = jnp.where(lane == index, 1.0, 0.0).astype(BF16)
        _, short = row_facts(lens, dest, group ^ (block >> 1), group, rows, slot)
        first = short[0][2]
        second = first + short[1][2]
        begin = jnp.where(column < first, 0, jnp.where(column < second, first, second))
        place_in_row = column - jnp.where((block & 1) == 1, begin, 0)
        pos[...] = jnp.broadcast_to(place_in_row.astype(F32), pos.shape)

    taken = dot(pick[...], home[...], NT)
    half = 2 * slot
    keep[...] = taken[:half].astype(BF16)
    send[...] = taken[half:].astype(BF16)


def deal(place, lens, dest, home, rows, slot):
    features = home.shape[0]
    width = min(features, 512)
    tokens = BLOCKS * slot
    return pl.pallas_call(
        functools.partial(deal_kernel, rows, slot),
        grid=(features // width,),
        in_specs=[
            in_smem(),
            in_smem(),
            in_smem(),
            pl.BlockSpec((width, home.shape[1]), lambda i: (i, 0)),
        ],
        out_specs=[
            pl.BlockSpec((tokens // 2, width), lambda i: (0, i)),
            pl.BlockSpec((tokens // 2, width), lambda i: (0, i)),
            pl.BlockSpec((slot, 128), lambda i: (0, 0)),
        ],
        out_shape=[
            jax.ShapeDtypeStruct((tokens // 2, features), BF16),
            jax.ShapeDtypeStruct((tokens // 2, features), BF16),
            jax.ShapeDtypeStruct((slot, 128), F32),
        ],
        scratch_shapes=[
            pltpu.VMEM((tokens, rows * slot), BF16),
        ],
        compiler_params=pltpu.CompilerParams(vmem_limit_bytes=ALL),
        name="deal",
    )(place, lens, dest, home)


def collect_kernel(count, extra, *refs):
    tokens, pieces = refs[:4], refs[4 : 4 + count]
    out, sums = refs[4 + count + extra : 6 + count + extra]
    x_buf, buf, x_sems, sems, out_sems = refs[-5:]
    copies = start_copies([(ref, buf.at[k]) for k, ref in enumerate(pieces)], sems)
    x_copies = start_copies([(ref, x_buf.at[i]) for i, ref in enumerate(tokens)], x_sems)
    sent = []
    for k, copy in enumerate(copies):
        copy.wait()
        sent += start_copies([(buf.at[k], out.at[k])], out_sems, k)
    _, half, features = x_buf.shape
    for i in range(2):
        total = None
        for j in (i, i + 2):
            x_copies[j].wait()
            for at in range(features // 128):
                piece = x_buf[j, :, at * 128 : (at + 1) * 128].astype(F32)
                total = piece * piece if total is None else total + piece * piece
        sums[:, i * half : (i + 1) * half] = jnp.broadcast_to(
            jnp.sum(total.T, axis=0, keepdims=True), (8, half)
        )
    for copy in sent:
        copy.wait()


def collect(tokens, pieces, after):
    count = len(pieces)
    half, features = tokens[0].shape
    return pl.pallas_call(
        functools.partial(collect_kernel, count, len(after)),
        in_specs=[anywhere()] * (4 + count + len(after)),
        out_specs=[anywhere(), in_vmem()],
        out_shape=[
            jax.ShapeDtypeStruct((count, *pieces[0].shape), BF16),
            jax.ShapeDtypeStruct((8, 2 * half), F32),
        ],
        scratch_shapes=[
            pltpu.VMEM((4, half, features), BF16),
            pltpu.VMEM((count, *pieces[0].shape), BF16),
            pltpu.SemaphoreType.DMA((4,)),
            pltpu.SemaphoreType.DMA((count,)),
            pltpu.SemaphoreType.DMA((count,)),
        ],
        compiler_params=pltpu.CompilerParams(vmem_limit_bytes=ALL),
        name="collect",
    )(*tokens, *pieces, *after)


def gate_kernel(*refs):
    pass


def gate(through, after):
    count = len(through)
    return pl.pallas_call(
        gate_kernel,
        in_specs=[anywhere()] * (count + len(after)),
        out_specs=[anywhere()] * count,
        out_shape=[jax.ShapeDtypeStruct(value.shape, value.dtype) for value in through],
        input_output_aliases={i: i for i in range(count)},
        compiler_params=pltpu.CompilerParams(vmem_limit_bytes=VMEM),
        name="gate",
    )(*through, *after)


def normalize_kernel(units, place, *rest):
    squares, (gain, keep, got, keep2, got2) = rest[:units], rest[units : units + 5]
    out, x_buf, normed, x_sems, out_sems = rest[units + 5 :]
    side = place[SIDE]
    _, half, features = x_buf.shape
    copies = start_copies(
        [(ref, x_buf.at[i]) for i, ref in enumerate((keep, got, keep2, got2))], x_sems
    )
    total = squares[0][...]
    for ref in squares[1:]:
        total = total + ref[...]
    inverse = lax.rsqrt(total / D + epsilon).T[:, :1]
    sent = []
    for i in range(4):
        at = side if i < 2 else 1 - side
        lanes = aligned(at * features, features)
        rows = slice((i & 1) * half, ((i & 1) + 1) * half)
        copies[i].wait()
        wide_rows = x_buf[i].astype(F32)
        normed[i] = (wide_rows * inverse[rows] * gain[:, lanes]).astype(BF16)
        sent += start_copies([(normed.at[i], out.at[rows, lanes])], out_sems, i)
    for copy in sent:
        copy.wait()


def normalize(place, squares, gain, keep, got, keep2, got2):
    half, features = keep.shape
    return pl.pallas_call(
        functools.partial(normalize_kernel, len(squares)),
        in_specs=[in_smem()] + [in_vmem()] * (len(squares) + 1) + [anywhere()] * 4,
        out_specs=anywhere(),
        out_shape=jax.ShapeDtypeStruct((2 * half, 2 * features), BF16),
        scratch_shapes=[
            pltpu.VMEM((4, half, features), BF16),
            pltpu.VMEM((4, half, features), BF16),
            pltpu.SemaphoreType.DMA((4,)),
            pltpu.SemaphoreType.DMA((4,)),
        ],
        compiler_params=pltpu.CompilerParams(vmem_limit_bytes=VMEM),
        name="normalize",
    )(place, *squares, gain, keep, got, keep2, got2)


def project_kernel(units, place, tokens, *rest):
    own_pieces, weights, outs = rest[:4], rest[4:8], rest[8:12]
    buf, out_sems = rest[12:]
    unit, quarter = place[UNIT], place[QUARTER]
    count, wide = tokens.shape
    slot = count // BLOCKS
    rows, own = own_pieces[0].shape
    size = wide // 4
    width = min(size, own)
    part = (rows - size) // (size // width)

    def weight(k, r, rows, lanes=slice(None)):
        return weights[r][k - 1, rows, lanes] if k else own_pieces[r][rows, lanes]

    def features(r, first, count):
        return tokens[:, aligned((quarter ^ r) * size + first, count)]

    sent = []

    def hand_out(group, cols, index, chunk, place_in_chunk):
        for k in range(4 * group, 4 * group + 4):
            rows = aligned(((unit ^ k) & 3) * slot, slot)
            target = outs[2 * chunk + (k & 1)].at[k >> 1, :, place_in_chunk]
            sent.extend(start_copies([(buf.at[group, rows, cols], target)], out_sems, 3 * k + index))

    for group in range(units // BLOCKS):
        members = range(4 * group, 4 * group + 4)
        for k in members:
            s = (unit ^ k) & 3
            value = None
            for r in range(4):
                term = dot(features(r, 0, size), weight(k, r, slice(0, size)))
                value = term if value is None else value + term
            buf[group, :, aligned(s * own, own)] = value.astype(BF16)
        hand_out(group, slice(0, 2 * own), 0, 0, slice(0, 2 * own))
        hand_out(group, slice(2 * own, 4 * own), 1, 1, slice(0, 2 * own))
        value = None
        for r in range(4):
            for e in range(size // width):
                pieces = []
                for half in range(2):
                    first = size + e * part + half * (part // 2)
                    rows, lanes = slice(first, first + part // 2), slice(0, width)
                    for s in range(4):
                        k = 4 * group + ((unit & 3) ^ s)
                        piece = weights[r][jnp.maximum(k - 1, 0), rows, lanes]
                        if group == 0:
                            piece = jnp.where(k == 0, own_pieces[r][rows, lanes], piece)
                        pieces.append(piece)
                w = jnp.concatenate(pieces, axis=0)
                term = dot(features(r, e * width, width), w, NT)
                value = term if value is None else value + term
        buf[group, :, 4 * own :] = value.astype(BF16)
        cols = slice(4 * own, 4 * own + 4 * part)
        hand_out(group, cols, 2, 0, slice(2 * own, 2 * own + 4 * part))
    for copy in sent:
        copy.wait()


def project(place, normed, own_pieces, weights, units):
    tokens, wide = normed.shape
    slot = tokens // BLOCKS
    rows, own = own_pieces[0].shape
    size = wide // 4
    part = (rows - size) // (size // min(size, own))
    groups = units // BLOCKS
    outs = pl.pallas_call(
        functools.partial(project_kernel, units),
        in_specs=[in_smem()] + [in_vmem()] * 9,
        out_specs=[anywhere()] * 4,
        out_shape=[jax.ShapeDtypeStruct((units // 2, slot, 2 * own + 4 * part), BF16)] * 2
        + [jax.ShapeDtypeStruct((units // 2, slot, 2 * own), BF16)] * 2,
        scratch_shapes=[
            pltpu.VMEM((groups, tokens, 4 * own + 4 * part), BF16),
            pltpu.SemaphoreType.DMA((3 * units,)),
        ],
        compiler_params=pltpu.CompilerParams(vmem_limit_bytes=VMEM),
        name="project",
    )(place, normed, *own_pieces, *weights)
    return outs


def pair_sum_kernel(kept, got, *outs):
    for i, out in enumerate(outs):
        out[...] = (kept[i + 1].astype(F32) + got[i + 1].astype(F32)).astype(BF16)


def pair_sums(kept, got):
    count = kept.shape[0] - 1
    return pl.pallas_call(
        pair_sum_kernel,
        in_specs=[in_vmem()] * 2,
        out_specs=[in_vmem()] * count,
        out_shape=[jax.ShapeDtypeStruct(kept.shape[1:], BF16)] * count,
        compiler_params=pltpu.CompilerParams(vmem_limit_bytes=VMEM),
        name="pair_sums",
    )(kept, got)


def all_parts(refs, cols):
    kept, got = refs[:2]
    value = kept[0, :, cols].astype(F32) + got[0, :, cols].astype(F32)
    for ref in refs[2:]:
        value = value + ref[:, cols].astype(F32)
    return value.astype(BF16).astype(F32)


def key_value_kernel(count, cosine, sine, *refs):
    parts, out = refs[:count], refs[-1]
    wide = parts[0].shape[2]
    value = all_parts(parts, slice(wide - out.shape[1], wide))
    keys, values = value[:, :HD], value[:, HD:]
    part = HD // 4
    lane = lax.broadcasted_iota(jnp.int32, keys.shape, 1)
    odd = (lane & part) != 0
    swapped = jnp.where(odd, pltpu.roll(keys, part, 1), pltpu.roll(keys, HD - part, 1))
    out[:, :HD] = (keys * cosine[...] + swapped * sine[...]).astype(BF16)
    out[:, HD:] = values.astype(BF16)


def key_value(parts, cosine, sine, after):
    return pl.pallas_call(
        functools.partial(key_value_kernel, len(parts)),
        in_specs=[in_vmem()] * (2 + len(parts)) + [anywhere()] * len(after),
        out_specs=in_vmem(),
        out_shape=jax.ShapeDtypeStruct((parts[0].shape[1], parts[0].shape[2] // 3), BF16),
        compiler_params=pltpu.CompilerParams(vmem_limit_bytes=VMEM),
        name="key_value",
    )(cosine, sine, *parts, *after)


def query_kernel(count, cosine, sine, *refs):
    parts, out = refs[:count], refs[-1]
    cos, sin = cosine[...], sine[...]
    for head in range(out.shape[1] // HD):
        at = slice(head * HD, (head + 1) * HD)
        query = all_parts(parts, at)
        out[:, at] = (query * cos + pltpu.roll(query, HD // 2, 1) * sin).astype(BF16)


def queries(parts, cosine, sine, wide, after):
    return pl.pallas_call(
        functools.partial(query_kernel, len(parts)),
        in_specs=[in_vmem()] * (2 + len(parts)) + [anywhere()] * len(after),
        out_specs=in_vmem(),
        out_shape=jax.ShapeDtypeStruct((parts[0].shape[1], wide), BF16),
        compiler_params=pltpu.CompilerParams(vmem_limit_bytes=VMEM),
        name="queries",
    )(cosine, sine, *parts, *after)


def attend_kernel(kv_head, rows, slot, place, lens, dest, query, own_kv, other_kv, out):
    group, block, side = place[GROUP], place[UNIT] & (BLOCKS - 1), place[SIDE]
    _, short = row_facts(lens, dest, group ^ (block >> 1), group, rows, slot)
    many = (block & 1) == 1
    first = jnp.where(many, short[0][2], slot)
    second = jnp.where(many, first + short[1][2], slot)

    def segment(shape, axis):
        at = lax.broadcasted_iota(jnp.int32, shape, axis)
        return jnp.where(at >= first, 1, 0) + jnp.where(at >= second, 1, 0)

    shape = (slot, slot)
    allowed = jnp.logical_and(
        segment(shape, 0) == segment(shape, 1),
        lax.broadcasted_iota(jnp.int32, shape, 1) <= lax.broadcasted_iota(jnp.int32, shape, 0),
    )
    mine, theirs = own_kv[...].astype(F32), other_kv[...].astype(F32)
    even = jnp.where(side == 0, mine, theirs)
    odd = jnp.where(side == 0, theirs, mine)
    part = HD // 4

    def whole_head(index):
        pieces = []
        for b in range(2):
            at = slice((2 * index + b) * part, (2 * index + b + 1) * part)
            pieces += [even[:, at], odd[:, at]]
        return jnp.concatenate(pieces, axis=1).astype(BF16)

    key, value = whole_head(kv_head), whole_head(2 + kv_head)
    scale = 1.0 / math.sqrt(HD)
    for head in range(out.shape[1] // HD):
        at = slice(head * HD, (head + 1) * HD)
        scores = dot(query[:, at], key, NT) * scale
        scores = jnp.where(allowed, scores, -1e30)
        weights = jnp.exp(scores - jnp.max(scores, axis=1, keepdims=True))
        attention = (weights / jnp.sum(weights, axis=1, keepdims=True)).astype(BF16)
        out[:, at] = dot(attention, value).astype(BF16)


def attend(place, lens, dest, query, own_kv, other_kv, kv_head, rows, slot):
    return pl.pallas_call(
        functools.partial(attend_kernel, kv_head, rows, slot),
        in_specs=[in_smem()] * 3 + [in_vmem()] * 3,
        out_specs=in_vmem(),
        out_shape=jax.ShapeDtypeStruct(query.shape, BF16),
        compiler_params=pltpu.CompilerParams(vmem_limit_bytes=VMEM),
        name="attend",
    )(place, lens, dest, query, own_kv, other_kv)


def output_kernel(units, rows, slot, place, lens, dest, *refs):
    weights, contexts = refs[:4], refs[4 : 4 + 4 * units]
    out, context, weight, buf, order, c_sems, w_sems, out_sems = refs[4 + 4 * units :]
    unit, side, quarter, group = place[UNIT], place[SIDE], place[QUARTER], place[GROUP]
    part = weights[0].shape[2]
    own = 4 * part
    half = 2 * slot
    features = weight.shape[3]
    c_copies, w_copies = [], []
    for e, y in enumerate((side, 1 - side)):
        w_copies.append(
            start_copies(
                [
                    (weights[r].at[:, y], weight.at[e, :, aligned((quarter ^ r) * part, part)])
                    for r in range(4)
                ],
                w_sems,
                4 * e,
            )
        )
        pairs = []
        for k in range(units):
            source = unit ^ k
            at = aligned((source & 3) * slot, slot)
            for h in range(2):
                lanes = aligned((source >> 2) * 4 * own + h * 2 * own, 2 * own)
                pairs.append((contexts[(2 * h + e) * units + k], context.at[e, at, lanes]))
        c_copies.append(start_copies(pairs, c_sems, e * 2 * units))
    column = lax.broadcasted_iota(jnp.int32, (1, half), 1)
    row = lax.broadcasted_iota(jnp.int32, (half, half), 0)
    for turn in range(2):
        full, short = row_facts(lens, dest, group ^ turn, group, rows, slot)
        index = column - full[1]
        done = jnp.int32(0)
        for k in range(3):
            inside = jnp.logical_and(column >= short[k][1], column < short[k][1] + short[k][2])
            index = jnp.where(inside, slot + done + column - short[k][1], index)
            done = done + short[k][2]
        order[turn] = jnp.where(row == index, 1.0, 0.0).astype(BF16)
    sums = [None, None]
    sent = []
    for e in range(2):
        for copy in w_copies[e] + c_copies[e]:
            copy.wait()
        for turn in range(2):
            term = dot(
                context[e, turn * half : (turn + 1) * half],
                weight[e].reshape(units * own, features),
            )
            sums[turn] = term if e == 0 else sums[turn] + term
            if e:
                buf[turn] = dot(sums[turn].astype(BF16), order[turn], TN).astype(BF16)
                columns = aligned((group ^ turn) * half, half)
                sent += start_copies([(buf.at[turn], out.at[:, columns])], out_sems, turn)
    for copy in sent:
        copy.wait()


def output(place, lens, dest, weights, contexts, rows, slot):
    units, _, part, features = weights[0].shape
    tokens = BLOCKS * slot
    return pl.pallas_call(
        functools.partial(output_kernel, units, rows, slot),
        in_specs=[in_smem()] * 3 + [anywhere()] * (4 + len(contexts)),
        out_specs=anywhere(),
        out_shape=jax.ShapeDtypeStruct((features, tokens), BF16),
        scratch_shapes=[
            pltpu.VMEM((2, tokens, units * 4 * part), BF16),
            pltpu.VMEM((2, units, 4 * part, features), BF16),
            pltpu.VMEM((2, features, tokens // 2), BF16),
            pltpu.VMEM((2, tokens // 2, tokens // 2), BF16),
            pltpu.SemaphoreType.DMA((len(contexts),)),
            pltpu.SemaphoreType.DMA((8,)),
            pltpu.SemaphoreType.DMA((2,)),
        ],
        compiler_params=pltpu.CompilerParams(vmem_limit_bytes=VMEM),
        name="output",
    )(place, lens, dest, *weights, *contexts)


def swap(value, axis, mask=1):
    size = lax.axis_size(axis)
    return lax.ppermute(value, axis, [(i, i ^ mask) for i in range(size)])


def over_units(values):
    return [values[0]] + [swap(values[k], "tensor", 2 * k) for k in range(1, len(values))]


def all_quarters(value):
    across = swap(value, "parts")
    return [value, swap(value, "dp"), across, swap(across, "dp")]


def body(
    home,
    gain,
    q_values,
    q_scales,
    k_values,
    k_scales,
    v_values,
    v_scales,
    o_values,
    o_scales,
    row_lengths,
    row_dest,
):
    ranks = lax.axis_size("tensor")
    units = ranks // 2
    rank = lax.axis_index("tensor")
    unit, side = rank >> 1, rank & 1
    group = lax.axis_index("dp")
    quarter = (lax.axis_index("parts") & 1) * 2 + group
    features = home.shape[0]
    rows = row_lengths.shape[0] // 2
    slot = home.shape[1] // rows
    kv_head = rank * k_values.shape[0] // HD
    place = jnp.stack([jnp.asarray(v, jnp.int32) for v in (group, unit, side, quarter, kv_head)])

    keep, send, pos = deal(place, row_lengths, row_dest, home, rows, slot)
    pieces = weight_pieces(
        place, q_values, q_scales, k_values, k_scales, v_values, v_scales, units, [keep]
    )
    own_gain = lax.dynamic_slice_in_dim(
        gain.astype(F32), unit * 2 * features, 2 * features
    ).reshape(1, -1)
    frequency = rope_base ** (-2.0 * jnp.arange(HD // 2, dtype=F32) / HD)
    phases = pos[:, :1] * frequency[None, :]
    cosine, sine = jnp.cos(phases), jnp.sin(phases)
    part = HD // 4
    own_cos = lax.dynamic_slice_in_dim(cosine, side * part, part, 1)
    own_sin = lax.dynamic_slice_in_dim(sine, side * part, part, 1)
    own_cos = jnp.concatenate([own_cos] * 4, axis=1)
    own_sin = jnp.concatenate([-own_sin, own_sin] * 2, axis=1)
    wide_cos = jnp.concatenate([cosine, cosine], axis=1)
    wide_sin = jnp.concatenate([-sine, sine], axis=1)

    got = swap(send, "dp")
    o_pieces, o_made = output_pieces(place, o_values, o_scales, ranks, [got])
    keep2 = swap(keep, "tensor")
    got2 = lax.ppermute(
        send, ("dp", "tensor"), [(i, i ^ (ranks + 1)) for i in range(2 * ranks)]
    )
    own_piece, *pieces = over_units(pieces)
    own_pieces = [own_piece, swap(own_piece, "dp"), swap(own_piece, "parts")]
    collected, squares = collect(
        [keep, got, keep2, got2],
        pieces,
        [own_gain, own_cos, own_sin, wide_cos, wide_sin, o_made, *own_pieces[1:]],
    )

    squares = over_units([squares] * units)
    own_pieces.append(swap(own_pieces[2], "dp"))
    weights = [collected, swap(collected, "dp"), swap(collected, "parts")]
    (o_pieces,) = gate([o_pieces], squares[1:])
    o_moved = lax.all_to_all(o_pieces, "tensor", split_axis=0, concat_axis=0, tiled=True)
    normed = normalize(place, squares, own_gain, keep, got, keep2, got2)
    (weights[2],) = gate(weights[2:], [weights[1], own_pieces[3], normed])

    weights.append(swap(weights[2], "dp"))
    kept_a, near_a, kept_b, near_b = project(place, normed, own_pieces, weights, units)
    (o_moved,) = gate([o_moved], [kept_a])
    got_a = swap(near_a, "tensor", 2)
    (near_b,) = gate([near_b], [got_a])
    parts = []
    for kept, got in ((kept_a, got_a), (kept_b, swap(near_b, "tensor", 2))):
        sums = list(pair_sums(kept, got))
        far = [swap(value, "tensor", 4 * (i + 1)) for i, value in enumerate(sums)]
        parts.append([kept, got, *far])
    own_kv = key_value(parts[0], own_cos, own_sin, sums[:1])
    other_kv = swap(own_kv, "tensor")
    o_weights = [
        value.reshape(units, 2, *value.shape[1:]) for value in all_quarters(o_moved)
    ]
    contexts = []
    for h in range(2):
        query = queries(parts[h], wide_cos, wide_sin, near_b.shape[2], contexts[units : units + 1])
        context = attend(
            place, row_lengths, row_dest, query, own_kv, other_kv, h, rows, slot
        )
        mine, theirs = [context], [swap(context, "tensor")]
        for k in range(1, units):
            mine.append(swap(mine[k & (k - 1)], "tensor", 2 * (k & -k)))
            if k == 2:
                (mine[2],) = gate(mine[2:], [mine[1], theirs[0]])
        theirs += [swap(value, "tensor") for value in mine[1:]]
        contexts += mine + theirs
    return output(place, row_lengths, row_dest, o_weights, contexts, rows, slot)


def solution(mesh):
    in_specs = (
        P("tensor", ("parts", "dp")),
        P(),
        P(None, "tensor"),
        P(None, "tensor"),
        P("tensor", None),
        P(),
        P("tensor", None),
        P(),
        P("tensor", None),
        P("tensor", None),
        P("parts"),
        P("parts"),
    )
    out_specs = P("tensor", ("parts", "dp"))
    return jax.shard_map(body, mesh=mesh, in_specs=in_specs, out_specs=out_specs, check_vma=False)
```
